32 devices in a mesh: prompt: 2 (over x), sample: 8 (over z, y), width: 2 (over core).
Axes of the slice: x: 2, y: 2, z: 4, core: 2. Of those that a mesh axis runs over, the one named last changes fastest.
Arguments:
- embeddings: bfloat16 [32, 128, 1024], P(('prompt', 'sample'), None, 'width'), parts along dimension 0, may hold values from -24 to 24
- lengths: int32 [32], P(('prompt', 'sample')), parts along dimension 0, may hold values from 8 to 128, as said below
Outputs:
- fscore: float32 [32, 16], P(('prompt', 'sample', 'width')), parts along dimension 0
- utility: float32 [32], P(('prompt', 'sample', 'width')), parts along dimension 0
The draws below stay inside these ranges and needn't reach their ends.
There are 2 independent parts, one for each index of `prompt`. The reference program is written for one: setup_inputs(seed, part) draws one part's arguments, and reference() takes and returns one part's arrays. A program takes and returns all parts, laid end to end along the dimension named above; each array names one. Nothing has to cross between parts.
Inputs may be any that keep to these rules, and one draw needn't show every extreme that they name: `lengths`: some hypothesis has exactly 128 tokens and some exactly 8.
All inputs are finite; a program needn't handle non-finite values.
Results may differ from the reference program's by a relative error of at most 0.0003.
Values may be sent and summed in bfloat16 or wider, within the bound.
No kernel may reach another device: no remote copies, remote signals or barrier semaphores. Data moves between devices by JAX's collectives and lax.ppermute only.
A program may use at most 64 MiB of HBM per device.

```python
import jax
import jax.numpy as jnp
from jax import lax

E = 1024
L = 128
H = 16


vocab_count = 4096


def draw_embeddings(key, part):
    key = jax.random.fold_in(key, 11)
    key_source = jax.random.fold_in(key, 1)
    key_rate = jax.random.fold_in(key, 2)
    key_chance = jax.random.fold_in(key, 3)
    key_swap = jax.random.fold_in(key, 4)
    key_move = jax.random.fold_in(key, 5)
    key_vocab = jax.random.fold_in(key, 6)
    key_feature = jax.random.fold_in(key, 7)
    key_shared = jax.random.fold_in(key, 8)
    key_weight = jax.random.fold_in(key, 9)
    key_scale = jax.random.fold_in(key, 10)
    key_noise = jax.random.fold_in(key, 12)
    key_tilt = jax.random.fold_in(key, 13)
    source_ids = jax.random.randint(key_source, (2 * L,), 0, vocab_count)
    sub_rates = jax.random.randint(key_rate, (H, 1), 10, 41)
    chance = jax.random.randint(key_chance, (H, L), 0, 100)
    swapped = jax.random.randint(key_swap, (H, L), 0, vocab_count)
    move_draw = jax.random.randint(key_move, (H, L), 0, 20)
    jump_steps = jnp.where(move_draw == 0, 1, jnp.where(move_draw == 1, -1, 0)).astype(jnp.int32)
    offset = jnp.cumsum(jump_steps, axis=1).astype(jnp.int32)
    slot_index = jnp.arange(L).astype(jnp.int32)[None, :]
    source_pos = jnp.clip(slot_index + offset, 0, 2 * L - 1).astype(jnp.int32)
    token_ids = jnp.where(chance < sub_rates, swapped, source_ids[source_pos]).astype(jnp.int32)
    vocab_table = jnp.clip(jax.random.normal(key_vocab, (vocab_count, E), jnp.float32), -4.0, 4.0)
    fraction = jnp.arange(E).astype(jnp.float32) / (E - 1)
    jitter = jnp.exp(jax.random.uniform(key_feature, (E,), jnp.float32, jnp.log(0.7), jnp.log(1.4)))
    shared = jnp.clip(jax.random.normal(key_shared, (E,), jnp.float32), -4.0, 4.0) * fraction * fraction
    weight = jnp.exp(jax.random.uniform(key_weight, (H, 1, 1), jnp.float32, jnp.log(0.2), jnp.log(2.0)))
    token_scale = jnp.exp(jax.random.uniform(key_scale, (H, L, 1), jnp.float32, jnp.log(0.25), jnp.log(2.5)))
    tilt_log = jax.random.uniform(key_tilt, (H, L, 1), jnp.float32, jnp.log(0.4), jnp.log(2.5))
    tilt = jnp.exp(tilt_log * fraction[None, None, :])
    noise_draw = jnp.clip(0.6 * jax.random.normal(key_noise, (H, L, E), jnp.float32), -3.6, 3.6)
    rise = 5.0
    feature_scale = 0.5 * jnp.exp(jnp.log(rise) * fraction) * jitter
    inner_value = jnp.take(vocab_table, token_ids, axis=0) + noise_draw + weight * shared[None, None, :]
    values = jnp.clip(token_scale * tilt * feature_scale[None, None, :] * inner_value, -24.0, 24.0)
    return values.astype(jnp.bfloat16)


def draw_lengths(key, part):
    key = jax.random.fold_in(key, 23)
    key_len, key_long, key_short = jax.random.split(key, 3)
    drawn = jax.random.randint(key_len, (H,), 8, L + 1)
    longest = jax.random.randint(key_long, (), 0, H)
    shortest = (longest + 1 + jax.random.randint(key_short, (), 0, H - 1)) % H
    index = jnp.arange(H)
    drawn = jnp.where(index == longest, L, drawn)
    drawn = jnp.where(index == shortest, 8, drawn)
    return drawn.astype(jnp.int32)


def setup_inputs(seed: int = 0, part: int = 0) -> dict:
    arg_keys = jax.random.split(jax.random.key(seed), 3)
    own_keys = jax.random.split(jax.random.fold_in(arg_keys[2], part), 3)
    return {
        "embeddings": draw_embeddings(jax.random.fold_in(jax.random.fold_in(arg_keys[2], part), 71), part),
        "lengths": draw_lengths(jax.random.fold_in(jax.random.fold_in(arg_keys[2], part), 71), part),
    }


def bert_f(similar, query_len, refer_len):
    position = jnp.arange(similar.shape[-1]).astype(jnp.float32)
    query_mask = position[None, :] < query_len[:, None]
    refer_mask = position[None, :] < refer_len[:, None]
    by_rows = jnp.where(refer_mask[None, :, None, :], similar, -4.0)
    best_query = lax.optimization_barrier(jnp.max(by_rows, axis=3))
    precis = lax.optimization_barrier(jnp.sum(jnp.where(query_mask[:, None, :], best_query, 0.0), axis=2)) / query_len[:, None]
    by_cols = jnp.where(query_mask[:, None, :, None], similar, -4.0)
    best_refer = lax.optimization_barrier(jnp.max(by_cols, axis=2))
    recall = lax.optimization_barrier(jnp.sum(jnp.where(refer_mask[None, :, :], best_refer, 0.0), axis=2)) / refer_len[None, :]
    return 2.0 * precis * recall / jnp.maximum(precis + recall, 1.0)

def reference(embeddings, lengths):
    values = embeddings.astype(jnp.float32)
    sumsq = lax.optimization_barrier(jnp.sum(values * values, axis=-1))
    scale = lax.rsqrt(sumsq / E + 1e-06) / jnp.sqrt(jnp.float32(E))
    normed = (values * scale[:, :, None]).astype(jnp.bfloat16)
    normed_wide = normed.astype(jnp.float32)
    all_len = lengths.astype(jnp.float32)

    def one_row(pair):
        row_tokens, row_len = pair
        similar = jnp.einsum('ae,jbe->jab', row_tokens, normed_wide, precision=lax.Precision.HIGHEST)
        return bert_f(similar[None], row_len[None], all_len)[0]
    fscore = lax.map(one_row, (normed_wide, all_len))
    diagonal = jnp.diagonal(fscore)
    utility = (lax.optimization_barrier(jnp.sum(fscore, axis=1)) - diagonal) / (H - 1)
    return (fscore, utility)
```

```python
import functools
import math

import jax
import jax.numpy as jnp
from jax import lax
from jax.experimental import pallas as pl
from jax.experimental.pallas import tpu as pltpu
from jax.sharding import PartitionSpec as P

VMEM = pltpu.VMEM
SMEM = pltpu.SMEM


def normalise(first, second, width):
    a = first.astype(jnp.float32)
    b = second.astype(jnp.float32)
    sumsq = jnp.sum(a * a + b * b, axis=-1, keepdims=True)
    scale = lax.rsqrt(sumsq / width + 1e-06) / math.sqrt(width)
    return (a * scale).astype(jnp.bfloat16), (b * scale).astype(jnp.bfloat16)


def pair_f(similar, row_len, col_len):
    slots = similar.shape[0]
    rows = lax.broadcasted_iota(jnp.int32, (slots, 1), 0).astype(jnp.float32)
    cols = lax.broadcasted_iota(jnp.int32, (1, slots), 1).astype(jnp.float32)
    row_real = rows < row_len
    col_real = cols < col_len
    by_row = jnp.max(similar + jnp.where(col_real, 0.0, -8.0), axis=1, keepdims=True)
    by_col = jnp.max(similar + jnp.where(row_real, 0.0, -8.0), axis=0, keepdims=True)
    prec = jnp.sum(jnp.where(row_real, by_row, 0.0), axis=0, keepdims=True) / row_len
    recall = jnp.sum(jnp.where(col_real, by_col, 0.0), axis=1, keepdims=True) / col_len
    return 2.0 * prec * recall / jnp.maximum(prec + recall, 1.0)


def dot_nt(a, b):
    return lax.dot_general(a, b, (((1,), (1,)), ((), ())), preferred_element_type=jnp.float32)


def peers(chip, half):
    turn = jnp.where(chip < half, 2, 3)
    return chip ^ 1, chip ^ turn, chip ^ (half + 2)


def early_kernel(
    half, len_o, len_y, len_z, len_r, o0, o1, y0, y1, z0, z1, tokens, lens, local, to_z
):
    slots, feat = o0.shape[1], o0.shape[2]
    width = 2 * feat
    w = lax.axis_index("width")
    chip = lax.axis_index("sample")
    y_chip, z_chip, _ = peers(chip, half)
    for k, (a, b) in enumerate(((o0, o1), (y0, y1), (z0, z1))):
        for v in range(2):
            na, nb = normalise(a[v], b[v], width)
            tokens[2 * k + v, :, :feat] = na
            tokens[2 * k + v, :, feat:] = nb
    lanes = lax.broadcasted_iota(jnp.int32, lens.shape, 1)
    table = jnp.zeros(lens.shape, jnp.float32)
    for k, ref in enumerate((len_o, len_y, len_z, len_r)):
        for v in range(2):
            table = jnp.where(lanes == 2 * k + v, ref[v].astype(jnp.float32), table)
    lens[...] = table
    o_len = len_o[w].astype(jnp.float32)
    z_len = len_z[w].astype(jnp.float32)
    own = tokens[w]
    every = tokens[...].reshape(6 * slots, width)
    sim = dot_nt(own, every)
    out_lane = lax.broadcasted_iota(jnp.int32, local.shape, 1)
    row = jnp.zeros(local.shape, jnp.float32)
    for k, (ref, place) in enumerate(((len_o, chip), (len_y, y_chip), (len_z, z_chip))):
        for v in range(2):
            at = (2 * k + v) * slots
            f = pair_f(sim[:, at : at + slots], o_len, ref[v].astype(jnp.float32))
            row = jnp.where(out_lane == 2 * place + v, f, row)
    local[...] = row
    sim = dot_nt(tokens[4 + w], tokens[2:4].reshape(2 * slots, width))
    row = jnp.zeros(to_z.shape, jnp.float32)
    for v in range(2):
        f = pair_f(sim[:, v * slots : (v + 1) * slots], z_len, len_y[v].astype(jnp.float32))
        row = jnp.where(out_lane == 2 * y_chip + v, f, row)
    to_z[...] = row


def late_kernel(half, tokens, lens, local_in, to_z_in, r0, r1, local, to_z, to_r, normed):
    slots, feat = r0.shape[1], r0.shape[2]
    width = 2 * feat
    w = lax.axis_index("width")
    chip = lax.axis_index("sample")
    y_chip, z_chip, r_chip = peers(chip, half)
    for v in range(2):
        na, nb = normalise(r0[v], r1[v], width)
        normed[v, :, :feat] = na
        normed[v, :, feat:] = nb
    table = lens[...]
    length = [table[:, k : k + 1] for k in range(8)]

    def of_core(k):
        return jnp.where(w == 0, length[k], length[k + 1])

    out_lane = lax.broadcasted_iota(jnp.int32, local.shape, 1)
    both = normed[...].reshape(2 * slots, width)
    for source, row_len, base, out in (
        (w, of_core(0), local_in, local),
        (4 + w, of_core(4), to_z_in, to_z),
    ):
        sim = dot_nt(tokens[source], both)
        row = base[...]
        for v in range(2):
            f = pair_f(sim[:, v * slots : (v + 1) * slots], row_len, length[6 + v])
            row = jnp.where(out_lane == 2 * r_chip + v, f, row)
        out[...] = row
    sim = dot_nt(normed[w], tokens[2:6].reshape(4 * slots, width))
    row = jnp.zeros(to_r.shape, jnp.float32)
    for k, place in enumerate((y_chip, z_chip)):
        for v in range(2):
            at = (2 * k + v) * slots
            f = pair_f(sim[:, at : at + slots], of_core(6), length[2 + 2 * k + v])
            row = jnp.where(out_lane == 2 * place + v, f, row)
    to_r[...] = row


def cross_body(embeddings, lengths):
    count = lax.axis_size("sample")
    half = count // 2
    _, slots, feat = embeddings.shape
    hyps = 2 * count
    swap = [(0, 1), (1, 0)]
    y_route = [(i, i ^ 1) for i in range(count)]
    z_route = [(i, i ^ (2 if i < half else 3)) for i in range(count)]
    r_route = [(i, i ^ (half + 2)) for i in range(count)]

    def send(x, route):
        return lax.ppermute(x, "sample", route)

    def other(x):
        return lax.ppermute(x, "width", swap)

    r = send(embeddings, r_route)
    z = send(embeddings, z_route)
    y = send(embeddings, y_route)
    len_r = send(lengths, r_route)
    len_z = send(lengths, z_route)
    len_y = send(lengths, y_route)
    row = jax.ShapeDtypeStruct((1, hyps), jnp.float32)
    limit = pltpu.CompilerParams(vmem_limit_bytes=16 * 1024 * 1024)
    tokens, lens, local, to_z = pl.pallas_call(
        functools.partial(early_kernel, half),
        out_shape=(
            jax.ShapeDtypeStruct((6, slots, 2 * feat), jnp.bfloat16),
            jax.ShapeDtypeStruct((1, slots), jnp.float32),
            row,
            row,
        ),
        in_specs=[pl.BlockSpec(memory_space=SMEM)] * 4 + [pl.BlockSpec(memory_space=VMEM)] * 6,
        out_specs=[pl.BlockSpec(memory_space=VMEM)] * 4,
        compiler_params=limit,
        cost_estimate=pl.CostEstimate(
            flops=2 * 8 * slots * slots * 2 * feat, bytes_accessed=4 << 20, transcendentals=0
        ),
    )(lengths, len_y, len_z, len_r, *halves(embeddings, other), *halves(y, other), *halves(z, other))
    local, to_z, to_r = pl.pallas_call(
        functools.partial(late_kernel, half),
        out_shape=(row, row, row),
        in_specs=[pl.BlockSpec(memory_space=VMEM)] * 6,
        out_specs=[pl.BlockSpec(memory_space=VMEM)] * 3,
        scratch_shapes=[pltpu.VMEM((2, slots, 2 * feat), jnp.bfloat16)],
        compiler_params=limit,
        cost_estimate=pl.CostEstimate(
            flops=2 * 8 * slots * slots * 2 * feat, bytes_accessed=2 << 20, transcendentals=0
        ),
    )(tokens, lens, local, to_z, *halves(r, other))
    scores = local + send(to_z, z_route) + send(to_r, r_route)
    own = 2 * lax.axis_index("sample") + lax.axis_index("width")
    rest = jnp.where(jnp.arange(hyps)[None, :] == own, 0.0, scores)
    return scores, jnp.sum(rest, axis=1) / (hyps - 1)


def halves(x, other):
    back = other(x)
    return x, back


def from_behind(block, axis, distance):
    devices = range(lax.axis_size(axis))
    route = [((i - distance) % len(devices), i) for i in devices]
    return lax.ppermute(block, axis, route)


def bert_f(similar, query_len, refer_len):
    position = jnp.arange(similar.shape[-1]).astype(jnp.float32)
    query_mask = position[None, :] < query_len[:, None]
    refer_mask = position[None, :] < refer_len[:, None]
    by_rows = jnp.where(refer_mask[None, :, None, :], similar, -4.0)
    best_query = jnp.max(by_rows, axis=3)
    precis = (
        jnp.sum(jnp.where(query_mask[:, None, :], best_query, 0.0), axis=2) / query_len[:, None]
    )
    by_cols = jnp.where(query_mask[:, None, :, None], similar, -4.0)
    best_refer = jnp.max(by_cols, axis=2)
    recall = (
        jnp.sum(jnp.where(refer_mask[None, :, :], best_refer, 0.0), axis=2) / refer_len[None, :]
    )
    return 2.0 * precis * recall / jnp.maximum(precis + recall, 1.0)


def ring_body(embeddings, lengths):
    block_rows = embeddings.shape[0]
    feature_part = embeddings.shape[2]
    width_count = lax.axis_size("width")
    cycle_count = lax.axis_size("sample")
    full_width = feature_part * width_count
    width_index = lax.axis_index("width")
    cycle_index = lax.axis_index("sample")
    values = embeddings.astype(jnp.float32)
    sumsq = lax.psum(jnp.sum(values * values, axis=-1), "width")
    scale = lax.rsqrt(sumsq / full_width + 1e-06) / math.sqrt(full_width)
    normed = (values * scale[:, :, None]).astype(jnp.bfloat16)
    own_len = lengths.astype(jnp.bfloat16)
    my_rows = block_rows // width_count
    my_len = lax.dynamic_slice_in_dim(lengths, width_index * my_rows, my_rows, 0).astype(
        jnp.float32
    )
    total_rows = block_rows * cycle_count

    def process(scores, piece, piece_len, source):
        similar = lax.psum_scatter(
            jnp.einsum("iae,jbe->ijab", normed, piece, preferred_element_type=jnp.float32),
            "width",
            scatter_dimension=0,
            tiled=True,
        )
        block = bert_f(similar, my_len, piece_len.astype(jnp.float32))
        column = source * block_rows
        return lax.dynamic_update_slice(scores, block, (jnp.int32(0), column))

    scores = jnp.zeros((my_rows, total_rows), jnp.float32)
    scores = process(scores, normed, own_len, cycle_index)

    def turn_one(step_index, carry):
        scores, piece, piece_len = carry
        piece, piece_len = from_behind((piece, piece_len), "sample", 1)
        scores = process(scores, piece, piece_len, (cycle_index - step_index) % cycle_count)
        return (scores, piece, piece_len)

    carried = lax.fori_loop(1, cycle_count, turn_one, (scores, normed, own_len))
    scores = carried[0]
    row_global = (cycle_index * width_count + width_index) * my_rows + jnp.arange(my_rows)
    column_index = jnp.arange(total_rows)
    diagonal = jnp.sum(jnp.where(column_index[None, :] == row_global[:, None], scores, 0.0), axis=1)
    utility = (jnp.sum(scores, axis=1) - diagonal) / (total_rows - 1)
    return (scores, utility)


def solution(mesh):
    in_specs = (P(("prompt", "sample"), None, "width"), P(("prompt", "sample")))
    out_specs = (P(("prompt", "sample", "width"), None), P(("prompt", "sample", "width")))
    body = cross_body if mesh.shape["sample"] == 8 and mesh.shape["width"] == 2 else ring_body
    return jax.shard_map(body, mesh=mesh, in_specs=in_specs, out_specs=out_specs, check_vma=False)
```

```python
import functools
import math

import jax
import jax.numpy as jnp
from jax import lax
from jax.experimental import pallas as pl
from jax.experimental.pallas import tpu as pltpu
from jax.sharding import PartitionSpec as P

VMEM = pltpu.VMEM
SMEM = pltpu.SMEM


def normalise(first, second, width):
    a = first.astype(jnp.float32)
    b = second.astype(jnp.float32)
    sumsq = jnp.sum(a * a + b * b, axis=-1, keepdims=True)
    scale = lax.rsqrt(sumsq / width + 1e-06) / math.sqrt(width)
    return (a * scale).astype(jnp.bfloat16), (b * scale).astype(jnp.bfloat16)


def pair_f(similar, row_len, col_len):
    slots = similar.shape[0]
    rows = lax.broadcasted_iota(jnp.int32, (slots, 1), 0).astype(jnp.float32)
    cols = lax.broadcasted_iota(jnp.int32, (1, slots), 1).astype(jnp.float32)
    row_real = rows < row_len
    col_real = cols < col_len
    by_row = jnp.max(similar + jnp.where(col_real, 0.0, -8.0), axis=1, keepdims=True)
    by_col = jnp.max(similar + jnp.where(row_real, 0.0, -8.0), axis=0, keepdims=True)
    prec = jnp.sum(jnp.where(row_real, by_row, 0.0), axis=0, keepdims=True) / row_len
    recall = jnp.sum(jnp.where(col_real, by_col, 0.0), axis=1, keepdims=True) / col_len
    return 2.0 * prec * recall / jnp.maximum(prec + recall, 1.0)


def dot_nt(a, b):
    return lax.dot_general(a, b, (((1,), (1,)), ((), ())), preferred_element_type=jnp.float32)


def peers(chip, half):
    turn = jnp.where(chip < half, 2, 3)
    return chip ^ 1, chip ^ turn, chip ^ (half + 2)


def pack_kernel(lengths, block, packed, scalars, sems):
    rows = packed.shape[0] - 16
    body = pltpu.make_async_copy(block, packed.at[:rows], sems.at[0])
    body.start()
    tail = pltpu.make_async_copy(lengths, scalars, sems.at[1])
    tail.start()
    tail.wait()
    row = lax.broadcasted_iota(jnp.int32, (16, 1), 0)
    value = jnp.where(row == 0, scalars[0], scalars[1]).astype(jnp.float32)
    packed[rows:] = jnp.broadcast_to(value, (16, packed.shape[1])).astype(packed.dtype)
    body.wait()


def near_kernel(len_r, o0, o1, y0, y1, z0, z1, tokens):
    slots, feat = (o0.shape[0] - 16) // 2, o0.shape[1]
    tails = []
    for k, (a, b) in enumerate(((o0, o1), (y0, y1), (z0, z1))):
        for v in range(2):
            at = slice(v * slots, (v + 1) * slots)
            na, nb = normalise(a[at], b[at], 2 * feat)
            to = slice((2 * k + v) * slots, (2 * k + v + 1) * slots)
            tokens[to, :feat] = na
            tokens[to, feat:] = nb
        tails.append(a[2 * slots :, :128].astype(jnp.float32))
    row = lax.broadcasted_iota(jnp.int32, (16, 128), 0)
    table = jnp.where(row == 6, len_r[0], len_r[1]).astype(jnp.float32)
    for k, tail in enumerate(tails):
        for v in range(2):
            table = jnp.where(row == 2 * k + v, tail[v : v + 1], table)
    tokens[6 * slots :, :128] = table.astype(tokens.dtype)


def lengths_of(tokens):
    table = tokens[tokens.shape[0] - 16 :, :128].astype(jnp.float32)
    w = lax.axis_index("width")
    every = [table[k : k + 1, :1] for k in range(8)]
    return every, [jnp.where(w == 0, every[k], every[k + 1]) for k in range(0, 8, 2)]


def early_kernel(half, tokens, local, to_z):
    slots = (tokens.shape[0] - 16) // 6
    w = lax.axis_index("width")
    chip = lax.axis_index("sample")
    y_chip, z_chip, _ = peers(chip, half)
    length, mine = lengths_of(tokens)
    out_lane = lax.broadcasted_iota(jnp.int32, local.shape, 1)
    row = jnp.zeros(local.shape, jnp.float32)
    sim = dot_nt(tokens[pl.ds(w * slots, slots)], tokens[: 6 * slots])
    for k, place in enumerate((chip, y_chip, z_chip)):
        for v in range(2):
            at = (2 * k + v) * slots
            f = pair_f(sim[:, at : at + slots], mine[0], length[2 * k + v])
            row = jnp.where(out_lane == 2 * place + v, f, row)
    local[...] = row
    sim = dot_nt(tokens[pl.ds((4 + w) * slots, slots)], tokens[2 * slots : 4 * slots])
    row = jnp.zeros(to_z.shape, jnp.float32)
    for v in range(2):
        f = pair_f(sim[:, v * slots : (v + 1) * slots], mine[2], length[2 + v])
        row = jnp.where(out_lane == 2 * y_chip + v, f, row)
    to_z[...] = row


def late_kernel(half, tokens, local_in, to_z_in, r0, r1, local, to_z, to_r, normed):
    slots, feat = r0.shape[1], r0.shape[2]
    width = 2 * feat
    w = lax.axis_index("width")
    chip = lax.axis_index("sample")
    y_chip, z_chip, r_chip = peers(chip, half)
    for v in range(2):
        na, nb = normalise(r0[v], r1[v], width)
        normed[v * slots : (v + 1) * slots, :feat] = na
        normed[v * slots : (v + 1) * slots, feat:] = nb
    length, mine = lengths_of(tokens)
    out_lane = lax.broadcasted_iota(jnp.int32, local.shape, 1)
    for k, base, out in ((0, local_in, local), (2, to_z_in, to_z)):
        sim = dot_nt(tokens[pl.ds((2 * k + w) * slots, slots)], normed[...])
        row = base[...]
        for v in range(2):
            f = pair_f(sim[:, v * slots : (v + 1) * slots], mine[k], length[6 + v])
            row = jnp.where(out_lane == 2 * r_chip + v, f, row)
        out[...] = row
    sim = dot_nt(normed[pl.ds(w * slots, slots)], tokens[2 * slots : 6 * slots])
    row = jnp.zeros(to_r.shape, jnp.float32)
    for k, place in enumerate((y_chip, z_chip)):
        for v in range(2):
            at = (2 * k + v) * slots
            f = pair_f(sim[:, at : at + slots], mine[3], length[2 + 2 * k + v])
            row = jnp.where(out_lane == 2 * place + v, f, row)
    to_r[...] = row


def final_kernel(local, from_z, from_r, scores, utility):
    hyps = local.shape[1]
    own = 2 * lax.axis_index("sample") + lax.axis_index("width")
    row = local[...] + from_z[...] + from_r[...]
    scores[...] = row
    lane = lax.broadcasted_iota(jnp.int32, row.shape, 1)
    rest = jnp.where(lane == own, 0.0, row)
    utility[...] = jnp.sum(rest, axis=1, keepdims=True) / (hyps - 1)


def cross_body(embeddings, lengths):
    count = lax.axis_size("sample")
    half = count // 2
    _, slots, feat = embeddings.shape
    hyps = 2 * count
    swap = [(0, 1), (1, 0)]
    y_route = [(i, i ^ 1) for i in range(count)]
    z_route = [(i, i ^ (2 if i < half else 3)) for i in range(count)]
    r_route = [(i, i ^ (half + 2)) for i in range(count)]

    def send(x, route):
        return lax.ppermute(x, "sample", route)

    def other(x):
        return lax.ppermute(x, "width", swap)

    row = jax.ShapeDtypeStruct((1, hyps), jnp.float32)
    limit = pltpu.CompilerParams(vmem_limit_bytes=16 * 1024 * 1024)

    def call(kernel, arrays, outs, scratch=(), places=None):
        places = places or [VMEM] * len(arrays)
        return pl.pallas_call(
            kernel,
            out_shape=outs,
            in_specs=[pl.BlockSpec(memory_space=place) for place in places],
            out_specs=[pl.BlockSpec(memory_space=VMEM)] * len(outs),
            scratch_shapes=scratch,
            compiler_params=limit,
        )(*arrays)

    def near():
        (packed,) = call(
            pack_kernel,
            (lengths, embeddings.reshape(2 * slots, feat)),
            (jax.ShapeDtypeStruct((2 * slots + 16, feat), jnp.bfloat16),),
            [pltpu.SMEM((2,), jnp.int32), pltpu.SemaphoreType.DMA((2,))],
            [pl.ANY] * 2,
        )
        len_r = send(lengths, r_route)
        y = send(packed, y_route)
        z = send(packed, z_route)
        y, z, len_r = lax.optimization_barrier((y, z, len_r))
        (tokens,) = call(
            near_kernel,
            (len_r, packed, other(packed), y, other(y), z, other(z)),
            (jax.ShapeDtypeStruct((6 * slots + 16, 2 * feat), jnp.bfloat16),),
            places=[SMEM] + [VMEM] * 6,
        )
        return tokens

    def nothing():
        return jnp.zeros((6 * slots + 16, 2 * feat), jnp.bfloat16)

    r = send(embeddings, r_route)
    tokens = lax.cond(lengths[0] > 0, near, nothing)
    r, tokens = lax.optimization_barrier((r, tokens))
    local, to_z = call(functools.partial(early_kernel, half), (tokens,), (row, row))
    local, to_z, to_r = call(
        functools.partial(late_kernel, half),
        (tokens, local, to_z, r, other(r)),
        (row, row, row),
        [pltpu.VMEM((2 * slots, 2 * feat), jnp.bfloat16)],
    )
    one = jax.ShapeDtypeStruct((1, 1), jnp.float32)
    from_z, from_r = send(to_z, z_route), send(to_r, r_route)
    scores, utility = call(final_kernel, (local, from_z, from_r), (row, one))
    return scores, utility.reshape(1)


def from_behind(block, axis, distance):
    devices = range(lax.axis_size(axis))
    route = [((i - distance) % len(devices), i) for i in devices]
    return lax.ppermute(block, axis, route)


def bert_f(similar, query_len, refer_len):
    position = jnp.arange(similar.shape[-1]).astype(jnp.float32)
    query_mask = position[None, :] < query_len[:, None]
    refer_mask = position[None, :] < refer_len[:, None]
    by_rows = jnp.where(refer_mask[None, :, None, :], similar, -4.0)
    best_query = jnp.max(by_rows, axis=3)
    precis = (
        jnp.sum(jnp.where(query_mask[:, None, :], best_query, 0.0), axis=2) / query_len[:, None]
    )
    by_cols = jnp.where(query_mask[:, None, :, None], similar, -4.0)
    best_refer = jnp.max(by_cols, axis=2)
    recall = (
        jnp.sum(jnp.where(refer_mask[None, :, :], best_refer, 0.0), axis=2) / refer_len[None, :]
    )
    return 2.0 * precis * recall / jnp.maximum(precis + recall, 1.0)


def ring_body(embeddings, lengths):
    block_rows = embeddings.shape[0]
    feature_part = embeddings.shape[2]
    width_count = lax.axis_size("width")
    cycle_count = lax.axis_size("sample")
    full_width = feature_part * width_count
    width_index = lax.axis_index("width")
    cycle_index = lax.axis_index("sample")
    values = embeddings.astype(jnp.float32)
    sumsq = lax.psum(jnp.sum(values * values, axis=-1), "width")
    scale = lax.rsqrt(sumsq / full_width + 1e-06) / math.sqrt(full_width)
    normed = (values * scale[:, :, None]).astype(jnp.bfloat16)
    own_len = lengths.astype(jnp.bfloat16)
    my_rows = block_rows // width_count
    my_len = lax.dynamic_slice_in_dim(lengths, width_index * my_rows, my_rows, 0).astype(
        jnp.float32
    )
    total_rows = block_rows * cycle_count

    def process(scores, piece, piece_len, source):
        similar = lax.psum_scatter(
            jnp.einsum("iae,jbe->ijab", normed, piece, preferred_element_type=jnp.float32),
            "width",
            scatter_dimension=0,
            tiled=True,
        )
        block = bert_f(similar, my_len, piece_len.astype(jnp.float32))
        column = source * block_rows
        return lax.dynamic_update_slice(scores, block, (jnp.int32(0), column))

    scores = jnp.zeros((my_rows, total_rows), jnp.float32)
    scores = process(scores, normed, own_len, cycle_index)

    def turn_one(step_index, carry):
        scores, piece, piece_len = carry
        piece, piece_len = from_behind((piece, piece_len), "sample", 1)
        scores = process(scores, piece, piece_len, (cycle_index - step_index) % cycle_count)
        return (scores, piece, piece_len)

    carried = lax.fori_loop(1, cycle_count, turn_one, (scores, normed, own_len))
    scores = carried[0]
    row_global = (cycle_index * width_count + width_index) * my_rows + jnp.arange(my_rows)
    column_index = jnp.arange(total_rows)
    diagonal = jnp.sum(jnp.where(column_index[None, :] == row_global[:, None], scores, 0.0), axis=1)
    utility = (jnp.sum(scores, axis=1) - diagonal) / (total_rows - 1)
    return (scores, utility)


def solution(mesh):
    in_specs = (P(("prompt", "sample"), None, "width"), P(("prompt", "sample")))
    out_specs = (P(("prompt", "sample", "width"), None), P(("prompt", "sample", "width")))
    body = cross_body if mesh.shape["sample"] == 8 and mesh.shape["width"] == 2 else ring_body
    return jax.shard_map(body, mesh=mesh, in_specs=in_specs, out_specs=out_specs, check_vma=False)
```

```python
import functools
import math

import jax
import jax.numpy as jnp
from jax import lax
from jax.experimental import pallas as pl
from jax.experimental.pallas import tpu as pltpu
from jax.sharding import PartitionSpec as P

VMEM = pltpu.VMEM
SMEM = pltpu.SMEM


def normalise(first, second, width):
    a = first.astype(jnp.float32)
    b = second.astype(jnp.float32)
    sumsq = jnp.sum(a * a + b * b, axis=-1, keepdims=True)
    scale = lax.rsqrt(sumsq / width + 1e-06) / math.sqrt(width)
    return (a * scale).astype(jnp.bfloat16), (b * scale).astype(jnp.bfloat16)


def pair_f(similar, row_len, col_len):
    slots = similar.shape[0]
    rows = lax.broadcasted_iota(jnp.int32, (slots, 1), 0).astype(jnp.float32)
    cols = lax.broadcasted_iota(jnp.int32, (1, slots), 1).astype(jnp.float32)
    row_real = rows < row_len
    col_real = cols < col_len
    by_row = jnp.max(similar + jnp.where(col_real, 0.0, -8.0), axis=1, keepdims=True)
    by_col = jnp.max(similar + jnp.where(row_real, 0.0, -8.0), axis=0, keepdims=True)
    prec = jnp.sum(jnp.where(row_real, by_row, 0.0), axis=0, keepdims=True) / row_len
    recall = jnp.sum(jnp.where(col_real, by_col, 0.0), axis=1, keepdims=True) / col_len
    return 2.0 * prec * recall / jnp.maximum(prec + recall, 1.0)


def dot_nt(a, b):
    return lax.dot_general(a, b, (((1,), (1,)), ((), ())), preferred_element_type=jnp.float32)


def peers(chip, half):
    return chip ^ 1, chip ^ 2, chip ^ jnp.where(chip < half, half + 2, half)


def pack_kernel(lengths, block, packed, scalars, sems):
    rows = packed.shape[0] - 16
    body = pltpu.make_async_copy(block, packed.at[:rows], sems.at[0])
    body.start()
    tail = pltpu.make_async_copy(lengths, scalars, sems.at[1])
    tail.start()
    tail.wait()
    row = lax.broadcasted_iota(jnp.int32, (16, 1), 0)
    value = jnp.where(row == 0, scalars[0], scalars[1]).astype(jnp.float32)
    packed[rows:] = jnp.broadcast_to(value, (16, packed.shape[1])).astype(packed.dtype)
    body.wait()


def unpack(first, second, normed, slots, start=0):
    feat = first.shape[1]
    for at in range(0, 2 * slots, slots):
        a, b = normalise(first[at : at + slots], second[at : at + slots], 2 * feat)
        normed[start + at : start + at + slots, :feat] = a
        normed[start + at : start + at + slots, feat:] = b


def of_core(pair):
    return jnp.where(lax.axis_index("width") == 0, *pair)


def lengths_of(tokens):
    rows = tokens[tokens.shape[0] - 16 :, :128].astype(jnp.float32)
    every = [rows[k : k + 1, :1] for k in range(4)]
    return every[:2], every[2:]


def row_of(base, similar, row_len, blocks):
    slots = similar.shape[0]
    lane = lax.broadcasted_iota(jnp.int32, base.shape, 1)
    for k, (place, length) in enumerate(blocks):
        for v in range(2):
            at = (2 * k + v) * slots
            f = pair_f(similar[:, at : at + slots], row_len, length[v])
            base = jnp.where(lane == 2 * place + v, f, base)
    return base


def near_kernel(half, o0, o1, y0, y1, tokens, local):
    slots = (o0.shape[0] - 16) // 2
    w = lax.axis_index("width")
    chip = lax.axis_index("sample")
    y_chip, _, _ = peers(chip, half)
    unpack(o0, o1, tokens, slots)
    unpack(y0, y1, tokens, slots, 2 * slots)
    row = lax.broadcasted_iota(jnp.int32, (16, 128), 0)
    table = jnp.zeros(row.shape, jnp.float32)
    for v in range(2):
        for k, source in enumerate((o0, y0)):
            tail = source[2 * slots :, :128].astype(jnp.float32)
            table = jnp.where(row == 2 * k + v, tail[v : v + 1], table)
    tokens[4 * slots :, :128] = table.astype(tokens.dtype)
    len_o, len_y = lengths_of(tokens)
    similar = dot_nt(tokens[pl.ds(w * slots, slots)], tokens[: 4 * slots])
    blocks = ((chip, len_o), (y_chip, len_y))
    local[...] = row_of(jnp.zeros(local.shape, jnp.float32), similar, of_core(len_o), blocks)


def far_kernel(half, far_len, other_len, tokens, z0, z1, r0, r1, local, to_y, to_r, normed):
    slots = z0.shape[0] // 2
    w = lax.axis_index("width")
    chip = lax.axis_index("sample")
    y_chip, z_chip, r_chip = peers(chip, half)
    unpack(z0, z1, normed, slots)
    unpack(r0, r1, normed, slots, 2 * slots)
    len_o, len_y = lengths_of(tokens)
    len_z, len_r = (
        [jnp.where(w == 0, a[v], b[v]).astype(jnp.float32) for v in range(2)]
        for a, b in ((far_len, other_len), (other_len, far_len))
    )
    empty = jnp.zeros(local.shape, jnp.float32)
    far = ((z_chip, len_z), (r_chip, len_r))
    for k, (length, out) in enumerate(((len_o, local), (len_y, to_y))):
        mine = tokens[pl.ds((2 * k + w) * slots, slots)]
        out[...] = row_of(empty, dot_nt(mine, normed[...]), of_core(length), far)
    mine = normed[pl.ds((2 + w) * slots, slots)]
    near = ((chip, len_o), (y_chip, len_y))
    to_r[...] = row_of(empty, dot_nt(mine, tokens[: 4 * slots]), of_core(len_r), near)


def final_kernel(near, local, from_y, from_r, scores, utility):
    hyps = local.shape[1]
    own = 2 * lax.axis_index("sample") + lax.axis_index("width")
    row = near[...] + local[...] + from_y[...] + from_r[...]
    scores[...] = row
    lane = lax.broadcasted_iota(jnp.int32, row.shape, 1)
    rest = jnp.where(lane == own, 0.0, row)
    utility[...] = jnp.sum(rest, axis=1, keepdims=True) / (hyps - 1)


def cross_body(embeddings, lengths):
    count = lax.axis_size("sample")
    half = count // 2
    _, slots, feat = embeddings.shape
    hyps = 2 * count
    swap = [(0, 1), (1, 0)]
    y_route = [(i, i ^ 1) for i in range(count)]
    z_route = [(i, i ^ 2) for i in range(count)]
    r_route = [(i, i ^ (half if i < half else half + 2)) for i in range(count)]
    back_route = [(b, a) for a, b in r_route]

    def send(x, route):
        return lax.ppermute(x, "sample", route)

    def other(x):
        return lax.ppermute(x, "width", swap)

    row = jax.ShapeDtypeStruct((1, hyps), jnp.float32)
    limit = pltpu.CompilerParams(vmem_limit_bytes=16 * 1024 * 1024)

    def call(kernel, arrays, outs, scratch=(), places=None):
        places = places or [VMEM] * len(arrays)
        return pl.pallas_call(
            kernel,
            out_shape=outs,
            in_specs=[pl.BlockSpec(memory_space=place) for place in places],
            out_specs=[pl.BlockSpec(memory_space=VMEM)] * len(outs),
            scratch_shapes=scratch,
            compiler_params=limit,
        )(*arrays)

    def near():
        (packed,) = call(
            pack_kernel,
            (lengths, embeddings.reshape(2 * slots, feat)),
            (jax.ShapeDtypeStruct((2 * slots + 16, feat), jnp.bfloat16),),
            [pltpu.SMEM((2,), jnp.int32), pltpu.SemaphoreType.DMA((2,))],
            [pl.ANY] * 2,
        )
        y = send(packed, y_route)
        return call(
            functools.partial(near_kernel, half),
            (packed, other(packed), y, other(y)),
            (jax.ShapeDtypeStruct((4 * slots + 16, 2 * feat), jnp.bfloat16), row),
        )

    def nothing():
        return jax.tree.map(lambda x: jnp.zeros(x.shape, x.dtype), jax.eval_shape(near))

    far_route = [(2 * a, 2 * b) for a, b in z_route] + [(2 * a + 1, 2 * b + 1) for a, b in r_route]
    far_len = lax.ppermute(lengths, ("sample", "width"), far_route)
    block = embeddings.reshape(2 * slots, feat)
    z = send(block, z_route)
    r = send(block, r_route)
    tokens, near_row = lax.cond(lax.axis_index("sample") >= 0, near, nothing)
    tokens, z, r, far_len = lax.optimization_barrier((tokens, z, r, far_len))
    local, to_y, to_r = call(
        functools.partial(far_kernel, half),
        (far_len, other(far_len), tokens, z, other(z), r, other(r)),
        (row, row, row),
        [pltpu.VMEM((4 * slots, 2 * feat), jnp.bfloat16)],
        [SMEM] * 2 + [VMEM] * 5,
    )
    one = jax.ShapeDtypeStruct((1, 1), jnp.float32)
    from_y, from_r = send(to_y, y_route), send(to_r, back_route)
    scores, utility = call(final_kernel, (near_row, local, from_y, from_r), (row, one))
    return scores, utility.reshape(1)


def from_behind(block, axis, distance):
    devices = range(lax.axis_size(axis))
    route = [((i - distance) % len(devices), i) for i in devices]
    return lax.ppermute(block, axis, route)


def bert_f(similar, query_len, refer_len):
    position = jnp.arange(similar.shape[-1]).astype(jnp.float32)
    query_mask = position[None, :] < query_len[:, None]
    refer_mask = position[None, :] < refer_len[:, None]
    by_rows = jnp.where(refer_mask[None, :, None, :], similar, -4.0)
    best_query = jnp.max(by_rows, axis=3)
    precis = (
        jnp.sum(jnp.where(query_mask[:, None, :], best_query, 0.0), axis=2) / query_len[:, None]
    )
    by_cols = jnp.where(query_mask[:, None, :, None], similar, -4.0)
    best_refer = jnp.max(by_cols, axis=2)
    recall = (
        jnp.sum(jnp.where(refer_mask[None, :, :], best_refer, 0.0), axis=2) / refer_len[None, :]
    )
    return 2.0 * precis * recall / jnp.maximum(precis + recall, 1.0)


def ring_body(embeddings, lengths):
    block_rows = embeddings.shape[0]
    feature_part = embeddings.shape[2]
    width_count = lax.axis_size("width")
    cycle_count = lax.axis_size("sample")
    full_width = feature_part * width_count
    width_index = lax.axis_index("width")
    cycle_index = lax.axis_index("sample")
    values = embeddings.astype(jnp.float32)
    sumsq = lax.psum(jnp.sum(values * values, axis=-1), "width")
    scale = lax.rsqrt(sumsq / full_width + 1e-06) / math.sqrt(full_width)
    normed = (values * scale[:, :, None]).astype(jnp.bfloat16)
    own_len = lengths.astype(jnp.bfloat16)
    my_rows = block_rows // width_count
    my_len = lax.dynamic_slice_in_dim(lengths, width_index * my_rows, my_rows, 0).astype(
        jnp.float32
    )
    total_rows = block_rows * cycle_count

    def process(scores, piece, piece_len, source):
        similar = lax.psum_scatter(
            jnp.einsum("iae,jbe->ijab", normed, piece, preferred_element_type=jnp.float32),
            "width",
            scatter_dimension=0,
            tiled=True,
        )
        block = bert_f(similar, my_len, piece_len.astype(jnp.float32))
        column = source * block_rows
        return lax.dynamic_update_slice(scores, block, (jnp.int32(0), column))

    scores = jnp.zeros((my_rows, total_rows), jnp.float32)
    scores = process(scores, normed, own_len, cycle_index)

    def turn_one(step_index, carry):
        scores, piece, piece_len = carry
        piece, piece_len = from_behind((piece, piece_len), "sample", 1)
        scores = process(scores, piece, piece_len, (cycle_index - step_index) % cycle_count)
        return (scores, piece, piece_len)

    carried = lax.fori_loop(1, cycle_count, turn_one, (scores, normed, own_len))
    scores = carried[0]
    row_global = (cycle_index * width_count + width_index) * my_rows + jnp.arange(my_rows)
    column_index = jnp.arange(total_rows)
    diagonal = jnp.sum(jnp.where(column_index[None, :] == row_global[:, None], scores, 0.0), axis=1)
    utility = (jnp.sum(scores, axis=1) - diagonal) / (total_rows - 1)
    return (scores, utility)


def solution(mesh):
    in_specs = (P(("prompt", "sample"), None, "width"), P(("prompt", "sample")))
    out_specs = (P(("prompt", "sample", "width"), None), P(("prompt", "sample", "width")))
    body = cross_body if mesh.shape["sample"] == 8 and mesh.shape["width"] == 2 else ring_body
    return jax.shard_map(body, mesh=mesh, in_specs=in_specs, out_specs=out_specs, check_vma=False)
```

```python
import functools
import math

import jax
import jax.numpy as jnp
from jax import lax
from jax.experimental import pallas as pl
from jax.experimental.pallas import tpu as pltpu
from jax.sharding import PartitionSpec as P

VMEM = pltpu.VMEM
SMEM = pltpu.SMEM


def normalise(first, second, width):
    a = first.astype(jnp.float32)
    b = second.astype(jnp.float32)
    sumsq = jnp.sum(a * a + b * b, axis=-1, keepdims=True)
    scale = lax.rsqrt(sumsq / width + 1e-06) / math.sqrt(width)
    return (a * scale).astype(jnp.bfloat16), (b * scale).astype(jnp.bfloat16)


def pair_f(similar, row_len, col_len):
    slots = similar.shape[0]
    rows = lax.broadcasted_iota(jnp.int32, (slots, 1), 0).astype(jnp.float32)
    cols = lax.broadcasted_iota(jnp.int32, (1, slots), 1).astype(jnp.float32)
    row_real = rows < row_len
    col_real = cols < col_len
    by_row = jnp.max(similar + jnp.where(col_real, 0.0, -8.0), axis=1, keepdims=True)
    by_col = jnp.max(similar + jnp.where(row_real, 0.0, -8.0), axis=0, keepdims=True)
    prec = jnp.sum(jnp.where(row_real, by_row, 0.0), axis=0, keepdims=True) / row_len
    recall = jnp.sum(jnp.where(col_real, by_col, 0.0), axis=1, keepdims=True) / col_len
    return 2.0 * prec * recall / jnp.maximum(prec + recall, 1.0)


def dot_nt(a, b):
    return lax.dot_general(a, b, (((1,), (1,)), ((), ())), preferred_element_type=jnp.float32)


def peers(chip, half):
    return chip ^ 1, chip ^ 2, chip ^ jnp.where(chip < half, half + 2, half)


def pack_kernel(lengths, block, packed, scalars, sems):
    rows = packed.shape[0] - 16
    body = pltpu.make_async_copy(block, packed.at[:rows], sems.at[0])
    body.start()
    tail = pltpu.make_async_copy(lengths, scalars, sems.at[1])
    tail.start()
    tail.wait()
    row = lax.broadcasted_iota(jnp.int32, (16, 1), 0)
    value = jnp.where(row == 0, scalars[0], scalars[1]).astype(jnp.float32)
    packed[rows:] = jnp.broadcast_to(value, (16, packed.shape[1])).astype(packed.dtype)
    body.wait()


def unpack(first, second, normed, slots, places):
    feat = first.shape[1]
    w = lax.axis_index("width")
    for v, at in zip((w, 1 - w), places):
        rows = pl.ds(pl.multiple_of(v * slots, slots), slots)
        a, b = normalise(first[rows], second[rows], 2 * feat)
        normed[at : at + slots, :feat] = a
        normed[at : at + slots, feat:] = b


def of_cores(pair):
    w = lax.axis_index("width")
    return jnp.where(w == 0, pair[0], pair[1]), jnp.where(w == 0, pair[1], pair[0])


def lengths_of(tokens):
    rows = tokens[tokens.shape[0] - 16 :, :128].astype(jnp.float32)
    every = [rows[k : k + 1, :1] for k in range(4)]
    return of_cores(every[:2]), of_cores(every[2:])


def lanes_of(place):
    w = lax.axis_index("width")
    return 2 * place + w, 2 * place + 1 - w


def put(out, entries):
    lane = lax.broadcasted_iota(jnp.int32, out.shape, 1)
    row = jnp.zeros(out.shape, jnp.float32)
    for place, f in entries:
        row = jnp.where(lane == place, f, row)
    out[...] = row


def near_kernel(half, o0, o1, y0, y1, tokens, local):
    slots = (o0.shape[0] - 16) // 2
    chip = lax.axis_index("sample")
    y_chip, _, _ = peers(chip, half)
    unpack(o0, o1, tokens, slots, (0, 2 * slots))
    unpack(y0, y1, tokens, slots, (slots, 3 * slots))
    row = lax.broadcasted_iota(jnp.int32, (16, 128), 0)
    table = jnp.zeros(row.shape, jnp.float32)
    for k, source in enumerate((o0, y0)):
        tail = source[2 * slots :, :128].astype(jnp.float32)
        for v in range(2):
            table = jnp.where(row == 2 * k + v, tail[v : v + 1], table)
    tokens[4 * slots :, :128] = table.astype(tokens.dtype)
    len_o, len_y = lengths_of(tokens)
    similar = dot_nt(tokens[:slots], tokens[: 4 * slots])
    places = zip(zip(lanes_of(chip), lanes_of(y_chip)), zip(len_o, len_y))
    entries = []
    for lanes, lengths in places:
        for lane, length in zip(lanes, lengths):
            at = len(entries) * slots
            entries.append((lane, pair_f(similar[:, at : at + slots], len_o[0], length)))
    put(local, entries)


def far_kernel(half, far_len, other_len, tokens, z0, z1, r0, r1, local, to_y, to_r, normed):
    slots = z0.shape[0] // 2
    w = lax.axis_index("width")
    chip = lax.axis_index("sample")
    y_chip, z_chip, r_chip = peers(chip, half)
    unpack(z0, z1, normed, slots, (0, slots))
    unpack(r0, r1, normed, slots, (2 * slots, 3 * slots))
    len_o, len_y = lengths_of(tokens)
    len_z, len_r = (
        of_cores([jnp.where(w == 0, a[v], b[v]).astype(jnp.float32) for v in range(2)])
        for a, b in ((far_len, other_len), (other_len, far_len))
    )
    similar = dot_nt(tokens[: 2 * slots], normed[...])
    col_len = (*len_z, *len_r)
    col_lane = (*lanes_of(z_chip), *lanes_of(r_chip))
    fs = []
    for k, length in enumerate((len_o[0], len_y[0])):
        rows = similar[k * slots : (k + 1) * slots]
        fs.append([pair_f(rows[:, n * slots : (n + 1) * slots], length, col_len[n]) for n in range(4)])
    similar = dot_nt(tokens[2 * slots : 4 * slots], normed[2 * slots : 3 * slots])
    rest = [
        pair_f(similar[k * slots : (k + 1) * slots], length, len_r[0])
        for k, length in enumerate((len_o[1], len_y[1]))
    ]
    put(local, zip(col_lane, fs[0]))
    put(to_y, zip(col_lane, fs[1]))
    near_lane = (*lanes_of(chip), *lanes_of(y_chip))
    put(to_r, zip(near_lane, (fs[0][2], rest[0], fs[1][2], rest[1])))


def final_kernel(near, local, from_y, from_r, scores, utility):
    hyps = local.shape[1]
    own = 2 * lax.axis_index("sample") + lax.axis_index("width")
    row = near[...] + local[...] + from_y[...] + from_r[...]
    scores[...] = row
    lane = lax.broadcasted_iota(jnp.int32, row.shape, 1)
    rest = jnp.where(lane == own, 0.0, row)
    utility[...] = jnp.sum(rest, axis=1, keepdims=True) / (hyps - 1)


def cross_body(embeddings, lengths):
    count = lax.axis_size("sample")
    half = count // 2
    _, slots, feat = embeddings.shape
    hyps = 2 * count
    swap = [(0, 1), (1, 0)]
    y_route = [(i, i ^ 1) for i in range(count)]
    z_route = [(i, i ^ 2) for i in range(count)]
    r_route = [(i, i ^ (half if i < half else half + 2)) for i in range(count)]
    back_route = [(b, a) for a, b in r_route]

    def send(x, route):
        return lax.ppermute(x, "sample", route)

    def other(x):
        return lax.ppermute(x, "width", swap)

    row = jax.ShapeDtypeStruct((1, hyps), jnp.float32)
    limit = pltpu.CompilerParams(vmem_limit_bytes=16 * 1024 * 1024)

    def call(kernel, arrays, outs, scratch=(), places=None):
        places = places or [VMEM] * len(arrays)
        return pl.pallas_call(
            kernel,
            out_shape=outs,
            in_specs=[pl.BlockSpec(memory_space=place) for place in places],
            out_specs=[pl.BlockSpec(memory_space=VMEM)] * len(outs),
            scratch_shapes=scratch,
            compiler_params=limit,
        )(*arrays)

    def near():
        (packed,) = call(
            pack_kernel,
            (lengths, embeddings.reshape(2 * slots, feat)),
            (jax.ShapeDtypeStruct((2 * slots + 16, feat), jnp.bfloat16),),
            [pltpu.SMEM((2,), jnp.int32), pltpu.SemaphoreType.DMA((2,))],
            [pl.ANY] * 2,
        )
        y = send(packed, y_route)
        return call(
            functools.partial(near_kernel, half),
            (packed, other(packed), y, other(y)),
            (jax.ShapeDtypeStruct((4 * slots + 16, 2 * feat), jnp.bfloat16), row),
        )

    def nothing():
        return jax.tree.map(lambda x: jnp.zeros(x.shape, x.dtype), jax.eval_shape(near))

    far_route = [(2 * a, 2 * b) for a, b in z_route] + [(2 * a + 1, 2 * b + 1) for a, b in r_route]
    far_len = lax.ppermute(lengths, ("sample", "width"), far_route)
    block = embeddings.reshape(2 * slots, feat)
    z = send(block, z_route)
    r = send(block, r_route)
    tokens, near_row = lax.cond(lax.axis_index("sample") >= 0, near, nothing)
    tokens, z, r, far_len = lax.optimization_barrier((tokens, z, r, far_len))
    local, to_y, to_r = call(
        functools.partial(far_kernel, half),
        (far_len, other(far_len), tokens, z, other(z), r, other(r)),
        (row, row, row),
        [pltpu.VMEM((4 * slots, 2 * feat), jnp.bfloat16)],
        [SMEM] * 2 + [VMEM] * 5,
    )
    one = jax.ShapeDtypeStruct((1, 1), jnp.float32)
    from_y, from_r = send(to_y, y_route), send(to_r, back_route)
    scores, utility = call(final_kernel, (near_row, local, from_y, from_r), (row, one))
    return scores, utility.reshape(1)


def from_behind(block, axis, distance):
    devices = range(lax.axis_size(axis))
    route = [((i - distance) % len(devices), i) for i in devices]
    return lax.ppermute(block, axis, route)


def bert_f(similar, query_len, refer_len):
    position = jnp.arange(similar.shape[-1]).astype(jnp.float32)
    query_mask = position[None, :] < query_len[:, None]
    refer_mask = position[None, :] < refer_len[:, None]
    by_rows = jnp.where(refer_mask[None, :, None, :], similar, -4.0)
    best_query = jnp.max(by_rows, axis=3)
    precis = (
        jnp.sum(jnp.where(query_mask[:, None, :], best_query, 0.0), axis=2) / query_len[:, None]
    )
    by_cols = jnp.where(query_mask[:, None, :, None], similar, -4.0)
    best_refer = jnp.max(by_cols, axis=2)
    recall = (
        jnp.sum(jnp.where(refer_mask[None, :, :], best_refer, 0.0), axis=2) / refer_len[None, :]
    )
    return 2.0 * precis * recall / jnp.maximum(precis + recall, 1.0)


def ring_body(embeddings, lengths):
    block_rows = embeddings.shape[0]
    feature_part = embeddings.shape[2]
    width_count = lax.axis_size("width")
    cycle_count = lax.axis_size("sample")
    full_width = feature_part * width_count
    width_index = lax.axis_index("width")
    cycle_index = lax.axis_index("sample")
    values = embeddings.astype(jnp.float32)
    sumsq = lax.psum(jnp.sum(values * values, axis=-1), "width")
    scale = lax.rsqrt(sumsq / full_width + 1e-06) / math.sqrt(full_width)
    normed = (values * scale[:, :, None]).astype(jnp.bfloat16)
    own_len = lengths.astype(jnp.bfloat16)
    my_rows = block_rows // width_count
    my_len = lax.dynamic_slice_in_dim(lengths, width_index * my_rows, my_rows, 0).astype(
        jnp.float32
    )
    total_rows = block_rows * cycle_count

    def process(scores, piece, piece_len, source):
        similar = lax.psum_scatter(
            jnp.einsum("iae,jbe->ijab", normed, piece, preferred_element_type=jnp.float32),
            "width",
            scatter_dimension=0,
            tiled=True,
        )
        block = bert_f(similar, my_len, piece_len.astype(jnp.float32))
        column = source * block_rows
        return lax.dynamic_update_slice(scores, block, (jnp.int32(0), column))

    scores = jnp.zeros((my_rows, total_rows), jnp.float32)
    scores = process(scores, normed, own_len, cycle_index)

    def turn_one(step_index, carry):
        scores, piece, piece_len = carry
        piece, piece_len = from_behind((piece, piece_len), "sample", 1)
        scores = process(scores, piece, piece_len, (cycle_index - step_index) % cycle_count)
        return (scores, piece, piece_len)

    carried = lax.fori_loop(1, cycle_count, turn_one, (scores, normed, own_len))
    scores = carried[0]
    row_global = (cycle_index * width_count + width_index) * my_rows + jnp.arange(my_rows)
    column_index = jnp.arange(total_rows)
    diagonal = jnp.sum(jnp.where(column_index[None, :] == row_global[:, None], scores, 0.0), axis=1)
    utility = (jnp.sum(scores, axis=1) - diagonal) / (total_rows - 1)
    return (scores, utility)


def solution(mesh):
    in_specs = (P(("prompt", "sample"), None, "width"), P(("prompt", "sample")))
    out_specs = (P(("prompt", "sample", "width"), None), P(("prompt", "sample", "width")))
    body = cross_body if mesh.shape["sample"] == 8 and mesh.shape["width"] == 2 else ring_body
    return jax.shard_map(body, mesh=mesh, in_specs=in_specs, out_specs=out_specs, check_vma=False)
```

```python
import functools
import math

import jax
import jax.numpy as jnp
from jax import lax
from jax.experimental import pallas as pl
from jax.experimental.pallas import tpu as pltpu
from jax.sharding import PartitionSpec as P

VMEM = pltpu.VMEM
SMEM = pltpu.SMEM


def normalise(first, second, width):
    a = first.astype(jnp.float32)
    b = second.astype(jnp.float32)
    sumsq = jnp.sum(a * a + b * b, axis=-1, keepdims=True)
    scale = lax.rsqrt(sumsq / width + 1e-06) / math.sqrt(width)
    return (a * scale).astype(jnp.bfloat16), (b * scale).astype(jnp.bfloat16)


def pair_f(similar, row_len, col_len):
    slots = similar.shape[0]
    rows = lax.broadcasted_iota(jnp.int32, (slots, 1), 0).astype(jnp.float32)
    cols = lax.broadcasted_iota(jnp.int32, (1, slots), 1).astype(jnp.float32)
    row_real = rows < row_len
    col_real = cols < col_len
    by_row = jnp.max(similar + jnp.where(col_real, 0.0, -8.0), axis=1, keepdims=True)
    by_col = jnp.max(similar + jnp.where(row_real, 0.0, -8.0), axis=0, keepdims=True)
    prec = jnp.sum(jnp.where(row_real, by_row, 0.0), axis=0, keepdims=True) / row_len
    recall = jnp.sum(jnp.where(col_real, by_col, 0.0), axis=1, keepdims=True) / col_len
    return 2.0 * prec * recall / jnp.maximum(prec + recall, 1.0)


def dot_nt(a, b):
    return lax.dot_general(a, b, (((1,), (1,)), ((), ())), preferred_element_type=jnp.float32)


def peers(chip, half):
    return chip ^ 1, chip ^ 2, chip ^ jnp.where(chip < half, half + 2, half)


def pack_kernel(lengths, block, packed, scalars, sems):
    rows = packed.shape[0] - 16
    body = pltpu.make_async_copy(block, packed.at[:rows], sems.at[0])
    body.start()
    tail = pltpu.make_async_copy(lengths, scalars, sems.at[1])
    tail.start()
    tail.wait()
    row = lax.broadcasted_iota(jnp.int32, (16, 1), 0)
    value = jnp.where(row == 0, scalars[0], scalars[1]).astype(jnp.float32)
    packed[rows:] = jnp.broadcast_to(value, (16, packed.shape[1])).astype(packed.dtype)
    body.wait()


def unpack(first, second, normed, slots, places):
    feat = first.shape[1]
    w = lax.axis_index("width")
    for v, at in zip((w, 1 - w), places):
        rows = pl.ds(pl.multiple_of(v * slots, slots), slots)
        a, b = normalise(first[rows], second[rows], 2 * feat)
        normed[at : at + slots, :feat] = a
        normed[at : at + slots, feat:] = b


def of_cores(pair):
    w = lax.axis_index("width")
    return jnp.where(w == 0, pair[0], pair[1]), jnp.where(w == 0, pair[1], pair[0])


def lengths_of(tokens):
    rows = tokens[tokens.shape[0] - 16 :, :128].astype(jnp.float32)
    every = [rows[k : k + 1, :1] for k in range(4)]
    return of_cores(every[:2]), of_cores(every[2:])


def lanes_of(place):
    w = lax.axis_index("width")
    return 2 * place + w, 2 * place + 1 - w


def put(out, entries, base=None):
    lane = lax.broadcasted_iota(jnp.int32, out.shape, 1)
    row = jnp.zeros(out.shape, jnp.float32) if base is None else base[...]
    for place, f in entries:
        row = jnp.where(lane == place, f, row)
    out[...] = row


def near_kernel(o0, o1, y0, y1, tokens):
    slots = (o0.shape[0] - 16) // 2
    unpack(o0, o1, tokens, slots, (0, 2 * slots))
    unpack(y0, y1, tokens, slots, (slots, 3 * slots))
    row = lax.broadcasted_iota(jnp.int32, (16, 128), 0)
    table = jnp.zeros(row.shape, jnp.float32)
    for k, source in enumerate((o0, y0)):
        tail = source[2 * slots :, :128].astype(jnp.float32)
        for v in range(2):
            table = jnp.where(row == 2 * k + v, tail[v : v + 1], table)
    tokens[4 * slots :, :128] = table.astype(tokens.dtype)


def pairs_kernel(half, tokens, local):
    slots = (tokens.shape[0] - 16) // 4
    chip = lax.axis_index("sample")
    y_chip, _, _ = peers(chip, half)
    len_o, len_y = lengths_of(tokens)
    similar = dot_nt(tokens[:slots], tokens[: 4 * slots])
    entries = []
    lanes = zip(lanes_of(chip), lanes_of(y_chip))
    for k, (lane, length) in enumerate(zip(sum(lanes, ()), sum(zip(len_o, len_y), ()))):
        f = pair_f(similar[:, k * slots : (k + 1) * slots], len_o[0], length)
        entries.append((lane, f))
    put(local, entries)


def far_length(far_len, other_len, core):
    mine = lax.axis_index("width") == core
    pair = [jnp.where(mine, far_len[v], other_len[v]).astype(jnp.float32) for v in range(2)]
    return of_cores(pair)


def z_kernel(half, far_len, other_len, tokens, z0, z1, local_in, local, to_y, normed):
    slots = z0.shape[0] // 2
    _, z_chip, _ = peers(lax.axis_index("sample"), half)
    unpack(z0, z1, normed, slots, (0, slots))
    len_o, len_y = lengths_of(tokens)
    len_z = far_length(far_len, other_len, 0)
    similar = dot_nt(tokens[: 2 * slots], normed[...])
    for k, (length, base, out) in enumerate(((len_o, local_in, local), (len_y, None, to_y))):
        rows = similar[k * slots : (k + 1) * slots]
        fs = [pair_f(rows[:, n * slots : (n + 1) * slots], length[0], len_z[n]) for n in range(2)]
        put(out, zip(lanes_of(z_chip), fs), base)


def r_kernel(
    half, far_len, other_len, tokens, r0, r1, local_in, to_y_in, local, to_y, to_r, normed
):
    slots = r0.shape[0] // 2
    chip = lax.axis_index("sample")
    y_chip, _, r_chip = peers(chip, half)
    unpack(r0, r1, normed, slots, (0, slots))
    len_o, len_y = lengths_of(tokens)
    len_r = far_length(far_len, other_len, 1)
    similar = dot_nt(tokens[: 2 * slots], normed[...])
    own = []
    for k, (length, base, out) in enumerate(((len_o, local_in, local), (len_y, to_y_in, to_y))):
        rows = similar[k * slots : (k + 1) * slots]
        fs = [pair_f(rows[:, n * slots : (n + 1) * slots], length[0], len_r[n]) for n in range(2)]
        put(out, zip(lanes_of(r_chip), fs), base)
        own.append(fs[0])
    similar = dot_nt(tokens[2 * slots : 4 * slots], normed[:slots])
    rest = [
        pair_f(similar[k * slots : (k + 1) * slots], length[1], len_r[0])
        for k, length in enumerate((len_o, len_y))
    ]
    near_lane = (*lanes_of(chip), *lanes_of(y_chip))
    put(to_r, zip(near_lane, (own[0], rest[0], own[1], rest[1])))


def final_kernel(local, from_y, from_r, scores, utility):
    hyps = local.shape[1]
    own = 2 * lax.axis_index("sample") + lax.axis_index("width")
    row = local[...] + from_y[...] + from_r[...]
    scores[...] = row
    lane = lax.broadcasted_iota(jnp.int32, row.shape, 1)
    rest = jnp.where(lane == own, 0.0, row)
    utility[...] = jnp.sum(rest, axis=1, keepdims=True) / (hyps - 1)


def cross_body(embeddings, lengths):
    count = lax.axis_size("sample")
    half = count // 2
    _, slots, feat = embeddings.shape
    hyps = 2 * count
    swap = [(0, 1), (1, 0)]
    y_route = [(i, i ^ 1) for i in range(count)]
    z_route = [(i, i ^ 2) for i in range(count)]
    r_route = [(i, i ^ (half if i < half else half + 2)) for i in range(count)]
    back_route = [(b, a) for a, b in r_route]

    def send(x, route):
        return lax.ppermute(x, "sample", route)

    def other(x):
        return lax.ppermute(x, "width", swap)

    row = jax.ShapeDtypeStruct((1, hyps), jnp.float32)
    limit = pltpu.CompilerParams(vmem_limit_bytes=16 * 1024 * 1024)

    def call(kernel, arrays, outs, scratch=(), places=None):
        places = places or [VMEM] * len(arrays)
        return pl.pallas_call(
            kernel,
            out_shape=outs,
            in_specs=[pl.BlockSpec(memory_space=place) for place in places],
            out_specs=[pl.BlockSpec(memory_space=VMEM)] * len(outs),
            scratch_shapes=scratch,
            compiler_params=limit,
        )(*arrays)

    def near():
        (packed,) = call(
            pack_kernel,
            (lengths, embeddings.reshape(2 * slots, feat)),
            (jax.ShapeDtypeStruct((2 * slots + 16, feat), jnp.bfloat16),),
            [pltpu.SMEM((2,), jnp.int32), pltpu.SemaphoreType.DMA((2,))],
            [pl.ANY] * 2,
        )
        y = send(packed, y_route)
        (tokens,) = call(
            near_kernel,
            (packed, other(packed), y, other(y)),
            (jax.ShapeDtypeStruct((4 * slots + 16, 2 * feat), jnp.bfloat16),),
        )
        return tokens

    def nothing():
        return jax.tree.map(lambda x: jnp.zeros(x.shape, x.dtype), jax.eval_shape(near))

    far_route = [(2 * a, 2 * b) for a, b in z_route] + [(2 * a + 1, 2 * b + 1) for a, b in r_route]
    far_len = lax.ppermute(lengths, ("sample", "width"), far_route)
    block = embeddings.reshape(2 * slots, feat)
    z = send(block, z_route)
    r = send(block, r_route)
    tokens = lax.cond(lax.axis_index("sample") >= 0, near, nothing)
    tokens, z, far_len = lax.optimization_barrier((tokens, z, far_len))
    z_other, far_other = other(z), other(far_len)
    (local,) = call(functools.partial(pairs_kernel, half), (tokens,), (row,))
    r, far_other, z_other, local = lax.optimization_barrier((r, far_other, z_other, local))
    scratch = [pltpu.VMEM((2 * slots, 2 * feat), jnp.bfloat16)]
    local, to_y = call(
        functools.partial(z_kernel, half),
        (far_len, far_other, tokens, z, z_other, local),
        (row, row),
        scratch,
        [SMEM] * 2 + [VMEM] * 4,
    )
    local, to_y, to_r = call(
        functools.partial(r_kernel, half),
        (far_len, far_other, tokens, r, other(r), local, to_y),
        (row, row, row),
        scratch,
        [SMEM] * 2 + [VMEM] * 5,
    )
    one = jax.ShapeDtypeStruct((1, 1), jnp.float32)
    from_r, from_y = send(to_r, back_route), send(to_y, y_route)
    scores, utility = call(final_kernel, (local, from_y, from_r), (row, one))
    return scores, utility.reshape(1)


def from_behind(block, axis, distance):
    devices = range(lax.axis_size(axis))
    route = [((i - distance) % len(devices), i) for i in devices]
    return lax.ppermute(block, axis, route)


def bert_f(similar, query_len, refer_len):
    position = jnp.arange(similar.shape[-1]).astype(jnp.float32)
    query_mask = position[None, :] < query_len[:, None]
    refer_mask = position[None, :] < refer_len[:, None]
    by_rows = jnp.where(refer_mask[None, :, None, :], similar, -4.0)
    best_query = jnp.max(by_rows, axis=3)
    precis = (
        jnp.sum(jnp.where(query_mask[:, None, :], best_query, 0.0), axis=2) / query_len[:, None]
    )
    by_cols = jnp.where(query_mask[:, None, :, None], similar, -4.0)
    best_refer = jnp.max(by_cols, axis=2)
    recall = (
        jnp.sum(jnp.where(refer_mask[None, :, :], best_refer, 0.0), axis=2) / refer_len[None, :]
    )
    return 2.0 * precis * recall / jnp.maximum(precis + recall, 1.0)


def ring_body(embeddings, lengths):
    block_rows = embeddings.shape[0]
    feature_part = embeddings.shape[2]
    width_count = lax.axis_size("width")
    cycle_count = lax.axis_size("sample")
    full_width = feature_part * width_count
    width_index = lax.axis_index("width")
    cycle_index = lax.axis_index("sample")
    values = embeddings.astype(jnp.float32)
    sumsq = lax.psum(jnp.sum(values * values, axis=-1), "width")
    scale = lax.rsqrt(sumsq / full_width + 1e-06) / math.sqrt(full_width)
    normed = (values * scale[:, :, None]).astype(jnp.bfloat16)
    own_len = lengths.astype(jnp.bfloat16)
    my_rows = block_rows // width_count
    my_len = lax.dynamic_slice_in_dim(lengths, width_index * my_rows, my_rows, 0).astype(
        jnp.float32
    )
    total_rows = block_rows * cycle_count

    def process(scores, piece, piece_len, source):
        similar = lax.psum_scatter(
            jnp.einsum("iae,jbe->ijab", normed, piece, preferred_element_type=jnp.float32),
            "width",
            scatter_dimension=0,
            tiled=True,
        )
        block = bert_f(similar, my_len, piece_len.astype(jnp.float32))
        column = source * block_rows
        return lax.dynamic_update_slice(scores, block, (jnp.int32(0), column))

    scores = jnp.zeros((my_rows, total_rows), jnp.float32)
    scores = process(scores, normed, own_len, cycle_index)

    def turn_one(step_index, carry):
        scores, piece, piece_len = carry
        piece, piece_len = from_behind((piece, piece_len), "sample", 1)
        scores = process(scores, piece, piece_len, (cycle_index - step_index) % cycle_count)
        return (scores, piece, piece_len)

    carried = lax.fori_loop(1, cycle_count, turn_one, (scores, normed, own_len))
    scores = carried[0]
    row_global = (cycle_index * width_count + width_index) * my_rows + jnp.arange(my_rows)
    column_index = jnp.arange(total_rows)
    diagonal = jnp.sum(jnp.where(column_index[None, :] == row_global[:, None], scores, 0.0), axis=1)
    utility = (jnp.sum(scores, axis=1) - diagonal) / (total_rows - 1)
    return (scores, utility)


def solution(mesh):
    in_specs = (P(("prompt", "sample"), None, "width"), P(("prompt", "sample")))
    out_specs = (P(("prompt", "sample", "width"), None), P(("prompt", "sample", "width")))
    body = cross_body if mesh.shape["sample"] == 8 and mesh.shape["width"] == 2 else ring_body
    return jax.shard_map(body, mesh=mesh, in_specs=in_specs, out_specs=out_specs, check_vma=False)
```

```python
import functools
import math

import jax
import jax.numpy as jnp
from jax import lax
from jax.experimental import pallas as pl
from jax.experimental.pallas import tpu as pltpu
from jax.sharding import PartitionSpec as P

VMEM = pltpu.VMEM
SMEM = pltpu.SMEM


def normalise(first, second, width):
    a = first.astype(jnp.float32)
    b = second.astype(jnp.float32)
    sumsq = jnp.sum(a * a + b * b, axis=-1, keepdims=True)
    scale = lax.rsqrt(sumsq / width + 1e-06) / math.sqrt(width)
    return (a * scale).astype(jnp.bfloat16), (b * scale).astype(jnp.bfloat16)


def pair_f(similar, row_len, col_len):
    slots = similar.shape[0]
    rows = lax.broadcasted_iota(jnp.int32, (slots, 1), 0).astype(jnp.float32)
    cols = lax.broadcasted_iota(jnp.int32, (1, slots), 1).astype(jnp.float32)
    row_real = rows < row_len
    col_real = cols < col_len
    by_row = jnp.max(similar + jnp.where(col_real, 0.0, -8.0), axis=1, keepdims=True)
    by_col = jnp.max(similar + jnp.where(row_real, 0.0, -8.0), axis=0, keepdims=True)
    prec = jnp.sum(jnp.where(row_real, by_row, 0.0), axis=0, keepdims=True) / row_len
    recall = jnp.sum(jnp.where(col_real, by_col, 0.0), axis=1, keepdims=True) / col_len
    return 2.0 * prec * recall / jnp.maximum(prec + recall, 1.0)


def dot_nt(a, b):
    return lax.dot_general(a, b, (((1,), (1,)), ((), ())), preferred_element_type=jnp.float32)


def peers(chip, half):
    return chip ^ 1, chip ^ 2, chip ^ jnp.where(chip < half, half + 2, half)


def pack_kernel(lengths, block, packed, scalars, sems):
    rows = packed.shape[0] - 16
    body = pltpu.make_async_copy(block, packed.at[:rows], sems.at[0])
    body.start()
    tail = pltpu.make_async_copy(lengths, scalars, sems.at[1])
    tail.start()
    tail.wait()
    row = lax.broadcasted_iota(jnp.int32, (16, 1), 0)
    value = jnp.where(row == 0, scalars[0], scalars[1]).astype(jnp.float32)
    packed[rows:] = jnp.broadcast_to(value, (16, packed.shape[1])).astype(packed.dtype)
    body.wait()


def unpack(first, second, normed, slots, places):
    feat = first.shape[1]
    w = lax.axis_index("width")
    for v, at in zip((w, 1 - w), places):
        rows = pl.ds(pl.multiple_of(v * slots, slots), slots)
        a, b = normalise(first[rows], second[rows], 2 * feat)
        normed[at : at + slots, :feat] = a
        normed[at : at + slots, feat:] = b


def of_cores(pair):
    w = lax.axis_index("width")
    return jnp.where(w == 0, pair[0], pair[1]), jnp.where(w == 0, pair[1], pair[0])


def lengths_of(tokens):
    rows = tokens[tokens.shape[0] - 16 :, :128].astype(jnp.float32)
    every = [rows[k : k + 1, :1] for k in range(4)]
    return of_cores(every[:2]), of_cores(every[2:])


def lanes_of(place):
    w = lax.axis_index("width")
    return 2 * place + w, 2 * place + 1 - w


def put(out, entries, base=None):
    lane = lax.broadcasted_iota(jnp.int32, out.shape, 1)
    row = jnp.zeros(out.shape, jnp.float32) if base is None else base[...]
    for place, f in entries:
        row = jnp.where(lane == place, f, row)
    out[...] = row


def near_kernel(o0, o1, y0, y1, tokens):
    slots = (o0.shape[0] - 16) // 2
    unpack(o0, o1, tokens, slots, (0, 2 * slots))
    unpack(y0, y1, tokens, slots, (slots, 3 * slots))
    row = lax.broadcasted_iota(jnp.int32, (16, 128), 0)
    table = jnp.zeros(row.shape, jnp.float32)
    for k, source in enumerate((o0, y0)):
        tail = source[2 * slots :, :128].astype(jnp.float32)
        for v in range(2):
            table = jnp.where(row == 2 * k + v, tail[v : v + 1], table)
    tokens[4 * slots :, :128] = table.astype(tokens.dtype)


def pairs_kernel(half, tokens, local):
    slots = (tokens.shape[0] - 16) // 4
    chip = lax.axis_index("sample")
    y_chip, _, _ = peers(chip, half)
    len_o, len_y = lengths_of(tokens)
    similar = dot_nt(tokens[:slots], tokens[: 4 * slots])
    entries = []
    lanes = zip(lanes_of(chip), lanes_of(y_chip))
    for k, (lane, length) in enumerate(zip(sum(lanes, ()), sum(zip(len_o, len_y), ()))):
        f = pair_f(similar[:, k * slots : (k + 1) * slots], len_o[0], length)
        entries.append((lane, f))
    put(local, entries)


def far_length(far_len, other_len, core):
    mine = lax.axis_index("width") == core
    pair = jnp.where(mine, far_len[...], other_len[...]).astype(jnp.float32)
    return of_cores([pair[:, v : v + 1] for v in range(2)])


def z_kernel(half, far_len, other_len, tokens, z0, z1, local_in, local, to_y, len_r, normed):
    slots = z0.shape[0] // 2
    _, z_chip, _ = peers(lax.axis_index("sample"), half)
    unpack(z0, z1, normed, slots, (0, slots))
    len_o, len_y = lengths_of(tokens)
    len_z = far_length(far_len, other_len, 0)
    for v, length in enumerate(far_length(far_len, other_len, 1)):
        len_r[v : v + 1] = jnp.broadcast_to(length, (1, len_r.shape[1]))
    similar = dot_nt(tokens[: 2 * slots], normed[...])
    for k, (length, base, out) in enumerate(((len_o, local_in, local), (len_y, None, to_y))):
        rows = similar[k * slots : (k + 1) * slots]
        fs = [pair_f(rows[:, n * slots : (n + 1) * slots], length[0], len_z[n]) for n in range(2)]
        put(out, zip(lanes_of(z_chip), fs), base)


def r_kernel(
    half, tokens, len_r, r0, r1, local_in, to_y_in, local, to_y, to_r, normed
):
    slots = r0.shape[0] // 2
    chip = lax.axis_index("sample")
    y_chip, _, r_chip = peers(chip, half)
    unpack(r0, r1, normed, slots, (0, slots))
    len_o, len_y = lengths_of(tokens)
    len_r = [len_r[v : v + 1, :1] for v in range(2)]
    similar = dot_nt(tokens[: 2 * slots], normed[...])
    own = []
    for k, (length, base, out) in enumerate(((len_o, local_in, local), (len_y, to_y_in, to_y))):
        rows = similar[k * slots : (k + 1) * slots]
        fs = [pair_f(rows[:, n * slots : (n + 1) * slots], length[0], len_r[n]) for n in range(2)]
        put(out, zip(lanes_of(r_chip), fs), base)
        own.append(fs[0])
    similar = dot_nt(tokens[2 * slots : 4 * slots], normed[:slots])
    rest = [
        pair_f(similar[k * slots : (k + 1) * slots], length[1], len_r[0])
        for k, length in enumerate((len_o, len_y))
    ]
    near_lane = (*lanes_of(chip), *lanes_of(y_chip))
    put(to_r, zip(near_lane, (own[0], rest[0], own[1], rest[1])))


def final_kernel(local, from_y, from_r, scores, utility):
    hyps = local.shape[1]
    own = 2 * lax.axis_index("sample") + lax.axis_index("width")
    row = local[...] + from_y[...] + from_r[...]
    scores[...] = row
    lane = lax.broadcasted_iota(jnp.int32, row.shape, 1)
    rest = jnp.where(lane == own, 0.0, row)
    utility[...] = jnp.sum(rest, axis=1, keepdims=True) / (hyps - 1)


def cross_body(embeddings, lengths):
    count = lax.axis_size("sample")
    half = count // 2
    _, slots, feat = embeddings.shape
    hyps = 2 * count
    swap = [(0, 1), (1, 0)]
    y_route = [(i, i ^ 1) for i in range(count)]
    z_route = [(i, i ^ 2) for i in range(count)]
    r_route = [(i, i ^ (half if i < half else half + 2)) for i in range(count)]
    back_route = [(b, a) for a, b in r_route]

    def send(x, route):
        return lax.ppermute(x, "sample", route)

    def other(x):
        return lax.ppermute(x, "width", swap)

    row = jax.ShapeDtypeStruct((1, hyps), jnp.float32)
    limit = pltpu.CompilerParams(vmem_limit_bytes=16 * 1024 * 1024)

    def call(kernel, arrays, outs, scratch=(), places=None):
        places = places or [VMEM] * len(arrays)
        return pl.pallas_call(
            kernel,
            out_shape=outs,
            in_specs=[pl.BlockSpec(memory_space=place) for place in places],
            out_specs=[pl.BlockSpec(memory_space=VMEM)] * len(outs),
            scratch_shapes=scratch,
            compiler_params=limit,
        )(*arrays)

    def near():
        (packed,) = call(
            pack_kernel,
            (lengths, embeddings.reshape(2 * slots, feat)),
            (jax.ShapeDtypeStruct((2 * slots + 16, feat), jnp.bfloat16),),
            [pltpu.SMEM((2,), jnp.int32), pltpu.SemaphoreType.DMA((2,))],
            [pl.ANY] * 2,
        )
        y = send(packed, y_route)
        (tokens,) = call(
            near_kernel,
            (packed, other(packed), y, other(y)),
            (jax.ShapeDtypeStruct((4 * slots + 16, 2 * feat), jnp.bfloat16),),
        )
        return tokens

    def nothing():
        return jax.tree.map(lambda x: jnp.zeros(x.shape, x.dtype), jax.eval_shape(near))

    far_route = [(2 * a, 2 * b) for a, b in z_route] + [(2 * a + 1, 2 * b + 1) for a, b in r_route]
    far_len = lax.ppermute(lengths.reshape(1, 2), ("sample", "width"), far_route)
    block = embeddings.reshape(2 * slots, feat)
    z = send(block, z_route)
    r = send(block, r_route)
    tokens = lax.cond(lax.axis_index("sample") >= 0, near, nothing)
    tokens, z, far_len = lax.optimization_barrier((tokens, z, far_len))
    z_other, far_other = other(z), other(far_len)
    (local,) = call(functools.partial(pairs_kernel, half), (tokens,), (row,))
    r, far_other, z_other, local = lax.optimization_barrier((r, far_other, z_other, local))
    scratch = [pltpu.VMEM((2 * slots, 2 * feat), jnp.bfloat16)]
    local, to_y, len_r = call(
        functools.partial(z_kernel, half),
        (far_len, far_other, tokens, z, z_other, local),
        (row, row, jax.ShapeDtypeStruct((2, 128), jnp.float32)),
        scratch,
    )
    local, to_y, to_r = call(
        functools.partial(r_kernel, half),
        (tokens, len_r, r, other(r), local, to_y),
        (row, row, row),
        scratch,
    )
    one = jax.ShapeDtypeStruct((1, 1), jnp.float32)
    from_r, from_y = send(to_r, back_route), send(to_y, y_route)
    scores, utility = call(final_kernel, (local, from_y, from_r), (row, one))
    return scores, utility.reshape(1)


def from_behind(block, axis, distance):
    devices = range(lax.axis_size(axis))
    route = [((i - distance) % len(devices), i) for i in devices]
    return lax.ppermute(block, axis, route)


def bert_f(similar, query_len, refer_len):
    position = jnp.arange(similar.shape[-1]).astype(jnp.float32)
    query_mask = position[None, :] < query_len[:, None]
    refer_mask = position[None, :] < refer_len[:, None]
    by_rows = jnp.where(refer_mask[None, :, None, :], similar, -4.0)
    best_query = jnp.max(by_rows, axis=3)
    precis = (
        jnp.sum(jnp.where(query_mask[:, None, :], best_query, 0.0), axis=2) / query_len[:, None]
    )
    by_cols = jnp.where(query_mask[:, None, :, None], similar, -4.0)
    best_refer = jnp.max(by_cols, axis=2)
    recall = (
        jnp.sum(jnp.where(refer_mask[None, :, :], best_refer, 0.0), axis=2) / refer_len[None, :]
    )
    return 2.0 * precis * recall / jnp.maximum(precis + recall, 1.0)


def ring_body(embeddings, lengths):
    block_rows = embeddings.shape[0]
    feature_part = embeddings.shape[2]
    width_count = lax.axis_size("width")
    cycle_count = lax.axis_size("sample")
    full_width = feature_part * width_count
    width_index = lax.axis_index("width")
    cycle_index = lax.axis_index("sample")
    values = embeddings.astype(jnp.float32)
    sumsq = lax.psum(jnp.sum(values * values, axis=-1), "width")
    scale = lax.rsqrt(sumsq / full_width + 1e-06) / math.sqrt(full_width)
    normed = (values * scale[:, :, None]).astype(jnp.bfloat16)
    own_len = lengths.astype(jnp.bfloat16)
    my_rows = block_rows // width_count
    my_len = lax.dynamic_slice_in_dim(lengths, width_index * my_rows, my_rows, 0).astype(
        jnp.float32
    )
    total_rows = block_rows * cycle_count

    def process(scores, piece, piece_len, source):
        similar = lax.psum_scatter(
            jnp.einsum("iae,jbe->ijab", normed, piece, preferred_element_type=jnp.float32),
            "width",
            scatter_dimension=0,
            tiled=True,
        )
        block = bert_f(similar, my_len, piece_len.astype(jnp.float32))
        column = source * block_rows
        return lax.dynamic_update_slice(scores, block, (jnp.int32(0), column))

    scores = jnp.zeros((my_rows, total_rows), jnp.float32)
    scores = process(scores, normed, own_len, cycle_index)

    def turn_one(step_index, carry):
        scores, piece, piece_len = carry
        piece, piece_len = from_behind((piece, piece_len), "sample", 1)
        scores = process(scores, piece, piece_len, (cycle_index - step_index) % cycle_count)
        return (scores, piece, piece_len)

    carried = lax.fori_loop(1, cycle_count, turn_one, (scores, normed, own_len))
    scores = carried[0]
    row_global = (cycle_index * width_count + width_index) * my_rows + jnp.arange(my_rows)
    column_index = jnp.arange(total_rows)
    diagonal = jnp.sum(jnp.where(column_index[None, :] == row_global[:, None], scores, 0.0), axis=1)
    utility = (jnp.sum(scores, axis=1) - diagonal) / (total_rows - 1)
    return (scores, utility)


def solution(mesh):
    in_specs = (P(("prompt", "sample"), None, "width"), P(("prompt", "sample")))
    out_specs = (P(("prompt", "sample", "width"), None), P(("prompt", "sample", "width")))
    body = cross_body if mesh.shape["sample"] == 8 and mesh.shape["width"] == 2 else ring_body
    return jax.shard_map(body, mesh=mesh, in_specs=in_specs, out_specs=out_specs, check_vma=False)
```

```python
import functools
import math

import jax
import jax.numpy as jnp
from jax import lax
from jax.experimental import pallas as pl
from jax.experimental.pallas import tpu as pltpu
from jax.sharding import PartitionSpec as P

VMEM = pltpu.VMEM
SMEM = pltpu.SMEM


def normalise(first, second, width):
    a = first.astype(jnp.float32)
    b = second.astype(jnp.float32)
    sumsq = jnp.sum(a * a + b * b, axis=-1, keepdims=True)
    scale = lax.rsqrt(sumsq / width + 1e-06) / math.sqrt(width)
    return (a * scale).astype(jnp.bfloat16), (b * scale).astype(jnp.bfloat16)


def pair_f(similar, row_len, col_len):
    slots = similar.shape[0]
    rows = lax.broadcasted_iota(jnp.int32, (slots, 1), 0).astype(jnp.float32)
    cols = lax.broadcasted_iota(jnp.int32, (1, slots), 1).astype(jnp.float32)
    row_real = rows < row_len
    col_real = cols < col_len
    by_row = jnp.max(similar + jnp.where(col_real, 0.0, -8.0), axis=1, keepdims=True)
    by_col = jnp.max(similar + jnp.where(row_real, 0.0, -8.0), axis=0, keepdims=True)
    prec = jnp.sum(jnp.where(row_real, by_row, 0.0), axis=0, keepdims=True) / row_len
    recall = jnp.sum(jnp.where(col_real, by_col, 0.0), axis=1, keepdims=True) / col_len
    return 2.0 * prec * recall / jnp.maximum(prec + recall, 1.0)


def dot_nt(a, b):
    return lax.dot_general(a, b, (((1,), (1,)), ((), ())), preferred_element_type=jnp.float32)


def peers(chip, half):
    return chip ^ 1, chip ^ 2, chip ^ jnp.where(chip < half, half + 2, half)


def pack_kernel(lengths, block, packed, scalars, sems):
    rows = packed.shape[0] - 16
    body = pltpu.make_async_copy(block, packed.at[:rows], sems.at[0])
    body.start()
    tail = pltpu.make_async_copy(lengths, scalars, sems.at[1])
    tail.start()
    tail.wait()
    row = lax.broadcasted_iota(jnp.int32, (16, 1), 0)
    value = jnp.where(row == 0, scalars[0], scalars[1]).astype(jnp.float32)
    packed[rows:] = jnp.broadcast_to(value, (16, packed.shape[1])).astype(packed.dtype)
    body.wait()


def unpack(first, second, normed, slots, places):
    feat = first.shape[1]
    w = lax.axis_index("width")
    for v, at in zip((w, 1 - w), places):
        rows = pl.ds(pl.multiple_of(v * slots, slots), slots)
        a, b = normalise(first[rows], second[rows], 2 * feat)
        normed[at : at + slots, :feat] = a
        normed[at : at + slots, feat:] = b


def of_cores(pair):
    w = lax.axis_index("width")
    return jnp.where(w == 0, pair[0], pair[1]), jnp.where(w == 0, pair[1], pair[0])


def lengths_of(tokens):
    rows = tokens[tokens.shape[0] - 16 :, :128].astype(jnp.float32)
    every = [rows[k : k + 1, :1] for k in range(4)]
    return of_cores(every[:2]), of_cores(every[2:])


def lanes_of(place):
    w = lax.axis_index("width")
    return 2 * place + w, 2 * place + 1 - w


def put(out, entries, base=None):
    lane = lax.broadcasted_iota(jnp.int32, out.shape, 1)
    row = jnp.zeros(out.shape, jnp.float32) if base is None else base[...]
    for place, f in entries:
        row = jnp.where(lane == place, f, row)
    out[...] = row


def near_kernel(o0, o1, y0, y1, tokens):
    slots = (o0.shape[0] - 16) // 2
    unpack(o0, o1, tokens, slots, (0, 2 * slots))
    unpack(y0, y1, tokens, slots, (slots, 3 * slots))
    row = lax.broadcasted_iota(jnp.int32, (16, 128), 0)
    table = jnp.zeros(row.shape, jnp.float32)
    for k, source in enumerate((o0, y0)):
        tail = source[2 * slots :, :128].astype(jnp.float32)
        for v in range(2):
            table = jnp.where(row == 2 * k + v, tail[v : v + 1], table)
    tokens[4 * slots :, :128] = table.astype(tokens.dtype)


def pairs_kernel(half, tokens, local):
    slots = (tokens.shape[0] - 16) // 4
    chip = lax.axis_index("sample")
    y_chip, _, _ = peers(chip, half)
    len_o, len_y = lengths_of(tokens)
    similar = dot_nt(tokens[:slots], tokens[: 4 * slots])
    entries = []
    lanes = zip(lanes_of(chip), lanes_of(y_chip))
    for k, (lane, length) in enumerate(zip(sum(lanes, ()), sum(zip(len_o, len_y), ()))):
        f = pair_f(similar[:, k * slots : (k + 1) * slots], len_o[0], length)
        entries.append((lane, f))
    put(local, entries)


def far_length(far_len, other_len, core):
    mine = lax.axis_index("width") == core
    pair = jnp.where(mine, far_len[...], other_len[...]).astype(jnp.float32)
    return of_cores([pair[:, v : v + 1] for v in range(2)])


def z_kernel(half, far_len, other_len, tokens, z0, z1, local_in, local, to_y, len_r, normed):
    slots = z0.shape[0] // 2
    _, z_chip, _ = peers(lax.axis_index("sample"), half)
    unpack(z0, z1, normed, slots, (0, slots))
    len_o, len_y = lengths_of(tokens)
    len_z = far_length(far_len, other_len, 0)
    for v, length in enumerate(far_length(far_len, other_len, 1)):
        len_r[v : v + 1] = jnp.broadcast_to(length, (1, len_r.shape[1]))
    similar = dot_nt(tokens[: 2 * slots], normed[...])
    for k, (length, base, out) in enumerate(((len_o, local_in, local), (len_y, None, to_y))):
        rows = similar[k * slots : (k + 1) * slots]
        fs = [pair_f(rows[:, n * slots : (n + 1) * slots], length[0], len_z[n]) for n in range(2)]
        put(out, zip(lanes_of(z_chip), fs), base)


def r_kernel(
    half, tokens, len_r, r0, r1, local_in, to_y_in, local, to_y, to_r, normed
):
    slots = r0.shape[0] // 2
    chip = lax.axis_index("sample")
    y_chip, _, r_chip = peers(chip, half)
    unpack(r0, r1, normed, slots, (0, slots))
    len_o, len_y = lengths_of(tokens)
    len_r = [len_r[v : v + 1, :1] for v in range(2)]
    similar = dot_nt(tokens[: 2 * slots], normed[...])
    own = []
    for k, (length, base, out) in enumerate(((len_o, local_in, local), (len_y, to_y_in, to_y))):
        rows = similar[k * slots : (k + 1) * slots]
        fs = [pair_f(rows[:, n * slots : (n + 1) * slots], length[0], len_r[n]) for n in range(2)]
        put(out, zip(lanes_of(r_chip), fs), base)
        own.append(fs[0])
    similar = dot_nt(tokens[2 * slots : 4 * slots], normed[:slots])
    rest = [
        pair_f(similar[k * slots : (k + 1) * slots], length[1], len_r[0])
        for k, length in enumerate((len_o, len_y))
    ]
    near_lane = (*lanes_of(chip), *lanes_of(y_chip))
    put(to_r, zip(near_lane, (own[0], rest[0], own[1], rest[1])))


def final_kernel(local, from_y, from_r, scores, utility):
    hyps = local.shape[1]
    own = 2 * lax.axis_index("sample") + lax.axis_index("width")
    row = local[...] + from_y[...] + from_r[...]
    scores[...] = row
    lane = lax.broadcasted_iota(jnp.int32, row.shape, 1)
    rest = jnp.where(lane == own, 0.0, row)
    utility[...] = jnp.sum(rest, axis=1, keepdims=True) / (hyps - 1)


def cross_body(embeddings, lengths):
    count = lax.axis_size("sample")
    half = count // 2
    _, slots, feat = embeddings.shape
    hyps = 2 * count
    swap = [(0, 1), (1, 0)]
    y_route = [(i, i ^ 1) for i in range(count)]
    z_route = [(i, i ^ 2) for i in range(count)]
    r_route = [(i, i ^ (half if i < half else half + 2)) for i in range(count)]
    back_route = [(b, a) for a, b in r_route]

    def send(x, route):
        return lax.ppermute(x, "sample", route)

    def other(x):
        return lax.ppermute(x, "width", swap)

    row = jax.ShapeDtypeStruct((1, hyps), jnp.float32)
    limit = pltpu.CompilerParams(vmem_limit_bytes=16 * 1024 * 1024)

    def call(kernel, arrays, outs, scratch=(), places=None):
        places = places or [VMEM] * len(arrays)
        return pl.pallas_call(
            kernel,
            out_shape=outs,
            in_specs=[pl.BlockSpec(memory_space=place) for place in places],
            out_specs=[pl.BlockSpec(memory_space=VMEM)] * len(outs),
            scratch_shapes=scratch,
            compiler_params=limit,
        )(*arrays)

    def near():
        (packed,) = call(
            pack_kernel,
            (lengths, embeddings.reshape(2 * slots, feat)),
            (jax.ShapeDtypeStruct((2 * slots + 16, feat), jnp.bfloat16),),
            [pltpu.SMEM((2,), jnp.int32), pltpu.SemaphoreType.DMA((2,))],
            [pl.ANY] * 2,
        )
        y = send(packed, y_route)
        (tokens,) = call(
            near_kernel,
            (packed, other(packed), y, other(y)),
            (jax.ShapeDtypeStruct((4 * slots + 16, 2 * feat), jnp.bfloat16),),
        )
        return tokens

    def nothing():
        return jax.tree.map(lambda x: jnp.zeros(x.shape, x.dtype), jax.eval_shape(near))

    far_route = [(2 * a, 2 * b) for a, b in z_route] + [(2 * a + 1, 2 * b + 1) for a, b in r_route]
    far_len = lax.ppermute(lengths.reshape(1, 2), ("sample", "width"), far_route)
    block = embeddings.reshape(2 * slots, feat)
    r = send(block, r_route)
    z = send(block, z_route)
    tokens = lax.cond(lax.axis_index("sample") >= 0, near, nothing)
    tokens, z, far_len = lax.optimization_barrier((tokens, z, far_len))
    z_other, far_other = other(z), other(far_len)
    (local,) = call(functools.partial(pairs_kernel, half), (tokens,), (row,))
    r, far_other, z_other, local = lax.optimization_barrier((r, far_other, z_other, local))
    scratch = [pltpu.VMEM((2 * slots, 2 * feat), jnp.bfloat16)]
    local, to_y, len_r = call(
        functools.partial(z_kernel, half),
        (far_len, far_other, tokens, z, z_other, local),
        (row, row, jax.ShapeDtypeStruct((2, 128), jnp.float32)),
        scratch,
    )
    local, to_y, to_r = call(
        functools.partial(r_kernel, half),
        (tokens, len_r, r, other(r), local, to_y),
        (row, row, row),
        scratch,
    )
    one = jax.ShapeDtypeStruct((1, 1), jnp.float32)
    from_y, from_r = send(to_y, y_route), send(to_r, back_route)
    scores, utility = call(final_kernel, (local, from_y, from_r), (row, one))
    return scores, utility.reshape(1)


def from_behind(block, axis, distance):
    devices = range(lax.axis_size(axis))
    route = [((i - distance) % len(devices), i) for i in devices]
    return lax.ppermute(block, axis, route)


def bert_f(similar, query_len, refer_len):
    position = jnp.arange(similar.shape[-1]).astype(jnp.float32)
    query_mask = position[None, :] < query_len[:, None]
    refer_mask = position[None, :] < refer_len[:, None]
    by_rows = jnp.where(refer_mask[None, :, None, :], similar, -4.0)
    best_query = jnp.max(by_rows, axis=3)
    precis = (
        jnp.sum(jnp.where(query_mask[:, None, :], best_query, 0.0), axis=2) / query_len[:, None]
    )
    by_cols = jnp.where(query_mask[:, None, :, None], similar, -4.0)
    best_refer = jnp.max(by_cols, axis=2)
    recall = (
        jnp.sum(jnp.where(refer_mask[None, :, :], best_refer, 0.0), axis=2) / refer_len[None, :]
    )
    return 2.0 * precis * recall / jnp.maximum(precis + recall, 1.0)


def ring_body(embeddings, lengths):
    block_rows = embeddings.shape[0]
    feature_part = embeddings.shape[2]
    width_count = lax.axis_size("width")
    cycle_count = lax.axis_size("sample")
    full_width = feature_part * width_count
    width_index = lax.axis_index("width")
    cycle_index = lax.axis_index("sample")
    values = embeddings.astype(jnp.float32)
    sumsq = lax.psum(jnp.sum(values * values, axis=-1), "width")
    scale = lax.rsqrt(sumsq / full_width + 1e-06) / math.sqrt(full_width)
    normed = (values * scale[:, :, None]).astype(jnp.bfloat16)
    own_len = lengths.astype(jnp.bfloat16)
    my_rows = block_rows // width_count
    my_len = lax.dynamic_slice_in_dim(lengths, width_index * my_rows, my_rows, 0).astype(
        jnp.float32
    )
    total_rows = block_rows * cycle_count

    def process(scores, piece, piece_len, source):
        similar = lax.psum_scatter(
            jnp.einsum("iae,jbe->ijab", normed, piece, preferred_element_type=jnp.float32),
            "width",
            scatter_dimension=0,
            tiled=True,
        )
        block = bert_f(similar, my_len, piece_len.astype(jnp.float32))
        column = source * block_rows
        return lax.dynamic_update_slice(scores, block, (jnp.int32(0), column))

    scores = jnp.zeros((my_rows, total_rows), jnp.float32)
    scores = process(scores, normed, own_len, cycle_index)

    def turn_one(step_index, carry):
        scores, piece, piece_len = carry
        piece, piece_len = from_behind((piece, piece_len), "sample", 1)
        scores = process(scores, piece, piece_len, (cycle_index - step_index) % cycle_count)
        return (scores, piece, piece_len)

    carried = lax.fori_loop(1, cycle_count, turn_one, (scores, normed, own_len))
    scores = carried[0]
    row_global = (cycle_index * width_count + width_index) * my_rows + jnp.arange(my_rows)
    column_index = jnp.arange(total_rows)
    diagonal = jnp.sum(jnp.where(column_index[None, :] == row_global[:, None], scores, 0.0), axis=1)
    utility = (jnp.sum(scores, axis=1) - diagonal) / (total_rows - 1)
    return (scores, utility)


def solution(mesh):
    in_specs = (P(("prompt", "sample"), None, "width"), P(("prompt", "sample")))
    out_specs = (P(("prompt", "sample", "width"), None), P(("prompt", "sample", "width")))
    body = cross_body if mesh.shape["sample"] == 8 and mesh.shape["width"] == 2 else ring_body
    return jax.shard_map(body, mesh=mesh, in_specs=in_specs, out_specs=out_specs, check_vma=False)
```
